1024 devices in a mesh: shard: 64 (over z, y), blk: 16 (over x, core).
Axes of the slice: x: 8, y: 8, z: 8, core: 2. Of those that a mesh axis runs over, the one named last changes fastest.
Arguments:
- item_feats: bfloat16 [131072, 2048], P(('shard', 'blk')), may hold values from -6 to 6
- owner: int32 [131072, 1], P(('shard', 'blk')), may hold values from 0 to 63; in each aligned block of 128 rows (0 to 127, 128 to 255, ...) at most 4 rows name the same one
- id_row: int32 [131072], P(('shard', 'blk')), may hold values from 0 to 1023
- counts: int32 [131072], P(('shard', 'blk')), may hold values from 3072 to 4096
- occurrence: int32 [262144], P(('shard', 'blk')), may hold values from 0 to 127
- users: bfloat16 [262144, 256], P(('shard', 'blk')), may hold values from -6 to 6
- w_first: bfloat16 [2048, 1024], replicated, may hold values from -0.125 to 0.125
- w_second: bfloat16 [1024, 256], replicated, may hold values from -0.1875 to 0.1875
- id_table: bfloat16 [65536, 1024], P('shard'), may hold values from -6 to 6
Outputs:
- loss: float32 [262144], P(('shard', 'blk'))
- user_grad: float32 [262144, 256], P(('shard', 'blk'))
- item_grad: float32 [131072, 256], P(('shard', 'blk'))
The draws below stay inside these ranges and needn't reach their ends.
Inputs may be any that keep to these rules, and one draw needn't show every extreme that they name: Among the unique items of one device no owner index appears more than 4 times, and some owner appears exactly 4 times.
All inputs are finite; a program needn't handle non-finite values.
Results may differ from the reference program's by a relative error of at most 0.012.
The reference program's roundings to bfloat16 on the way (of `rows`, `hidden`, `vecs`, `bias`, `unit_b` and `residue`) count: a program that leaves them out, or rounds other values in their place, can miss the bound.
Values may be sent and summed in bfloat16 or wider, within the bound.
No kernel may reach another device: no remote copies, remote signals or barrier semaphores. Data moves between devices by JAX's collectives and lax.ppermute only.
A program may use at most 32 MiB of HBM per device.

```python
import math
import jax
import jax.numpy as jnp
import numpy as np
from jax import lax

F = 2048
H = 1024
E = 256
U_DEV = 128
TAB_DEV = 1024
B_DEV = 256
CAP = 4
UNIQ = 131072
USERS = 262144
TABLE = 65536
N_SHARD = 64
N_BLK = 16


def with_ends(result, stream_key, smallest, largest):
    longest = result.shape.index(max(result.shape))
    spots = []
    for shift in (0, 1):
        where = [jax.random.randint(jax.random.fold_in(stream_key, axis), (), 0, length) for axis, length in enumerate(result.shape)]
        where[longest] = (where[longest] + shift) % result.shape[longest]
        spots.append(tuple(where))
    return result.at[spots[0]].set(smallest).at[spots[1]].set(largest)


def level_of(rng, extent, cuts, smallest, high):
    factor_of, own = 1.0, jax.random.fold_in(rng, 6)
    for position, parts in cuts:
        steps = jnp.exp(jax.random.uniform(jax.random.fold_in(own, position), (parts,), jnp.float32, smallest / len(cuts), high / len(cuts)))
        factor_of = factor_of * jnp.repeat(steps, extent[position] // parts).reshape([-1 if axis == position else 1 for axis in range(len(extent))])
    return factor_of


def deal_out(stream_key, own, number, rows, count, top, bound, lean):
    order = jax.random.permutation(stream_key, count)
    crowded, common = shares(count, rows * top, bound, lean, True), shares(count, rows * top, bound, lean, False)
    places = jnp.arange(count)

    def named(tallies, rotation):
        used = int((tallies > 0).sum())
        fixed = max(1, used // 4)
        passed = fixed + (places - fixed + rotation * (used - fixed)) % max(1, count - fixed)
        return jnp.zeros((count,), jnp.int32).at[order[jnp.where(places < fixed, places, passed)]].set(jnp.asarray(tallies, jnp.int32))

    tallies = jnp.where(number % 4 == 0, named(crowded, number // 4), named(common, number - number // 4 - 1))
    mixed = jax.random.permutation(jax.random.fold_in(own, 3), count)
    donor, sink = mixed[0:count // 2 * 2:2], mixed[1:count // 2 * 2:2]
    margin = jnp.minimum(tallies[donor] - 1, bound - tallies[sink]) // 2
    margin = jnp.where((donor == order[0]) | (sink == order[0]) | (tallies[sink] == 0), 0, jnp.maximum(margin, 0))
    passed = jax.random.randint(jax.random.fold_in(own, 4), (count // 2,), 0, 1 << 20) % (margin + 1)
    tallies = tallies.at[donor].add(-passed).at[sink].add(passed)
    labels = jnp.searchsorted(jnp.cumsum(tallies), jnp.arange(rows * top), side="right").astype(jnp.int32)
    table = labels.reshape(top, rows).T
    table = table[jax.random.permutation(jax.random.fold_in(own, 1), rows)]
    rotation = jax.random.randint(jax.random.fold_in(own, 2), (rows, 1), 0, top)
    return jnp.take_along_axis(table, (jnp.arange(top)[None, :] + rotation) % top, axis=1)


def shares(number_of, total, most, lean, full):
    loads = [(1 << 20) // math.isqrt(rank ** lean) + 1 for rank in range(1, number_of + 1)]
    largest = most if full else min(most, max(-(-total // number_of), total * loads[0] // sum(loads)))
    least = 1 if total - largest >= number_of - 1 else 0
    given, spare = [largest] + [least] * (number_of - 1), total - largest - least * (number_of - 1)
    while spare > 0:
        candidates = [i for i in range(1, number_of) if given[i] < largest] or [i for i in range(1, number_of) if given[i] < most]
        mass, left = sum([loads[i] for i in candidates]), spare
        for i in candidates:
            more = min(most - given[i], max(1, left * loads[i] // mass), spare)
            given[i] = given[i] + more
            spare = spare - more
    return np.array(given)


def scatter_about(rng, shape, width, limit, shards=(), kind=jnp.bfloat16):
    entries = jax.random.normal(rng, shape, jnp.float32) * width
    if len(shards) > 0:
        entries = level_of(rng, shape, shards, -0.22, 0.18) * entries
    return jnp.clip(entries, min=-limit, max=limit).astype(kind)


def setup_inputs(seed: int = 0) -> dict:
    key_of = jax.random.split(jax.random.key(seed), 10)
    item_feats = scatter_about(key_of[0], (UNIQ, F), 1.0, 6.0, ((0, 1024),))
    owner_keys = jax.random.split(jax.random.fold_in(key_of[1], 1), UNIQ // U_DEV)
    owner_turns = jax.random.permutation(jax.random.fold_in(key_of[1], 3), UNIQ // U_DEV)
    owner = jax.vmap(lambda own, number: deal_out(jax.random.fold_in(key_of[1], 2), own, number, U_DEV, N_SHARD, 1, CAP, 2))(owner_keys, owner_turns).reshape((UNIQ, 1))
    id_row = with_ends(jax.random.randint(key_of[2], (UNIQ,), 0, TAB_DEV), jax.random.fold_in(key_of[2], 1), 0, TAB_DEV - 1).astype(jnp.int32)
    counts = with_ends(jax.random.randint(key_of[3], (UNIQ,), 3072, 4097), jax.random.fold_in(key_of[3], 1), 3072, 4096).astype(jnp.int32)
    occurrence = with_ends(jax.random.randint(key_of[4], (USERS,), 0, U_DEV), jax.random.fold_in(key_of[4], 1), 0, U_DEV - 1).astype(jnp.int32)
    users = scatter_about(key_of[5], (USERS, E), 1.0, 6.0, ((0, 1024),))
    w_first = scatter_about(key_of[6], (F, H), F ** -0.5, 0.125)
    w_second = scatter_about(key_of[7], (H, E), H ** -0.5, 0.1875)
    id_table = scatter_about(key_of[8], (TABLE, H), 1.0, 6.0, ((0, 64),))
    return {"item_feats": item_feats, "owner": owner, "id_row": id_row, "counts": counts, "occurrence": occurrence, "users": users, "w_first": w_first, "w_second": w_second, "id_table": id_table}


logit_scale = 48.0

def encode_items(features, table_rows, w_first, w_second):
    pre = jnp.dot(features, w_first, preferred_element_type=jnp.float32) + table_rows.astype(jnp.float32)
    hidden = jnp.maximum(pre, 0.0).astype(jnp.bfloat16)
    emb = jnp.dot(hidden, w_second, preferred_element_type=jnp.float32)
    emb_square = lax.optimization_barrier(jnp.sum(emb * emb, -1, keepdims=True))
    return (emb * lax.rsqrt(emb_square + 1e-06)).astype(jnp.bfloat16)

def softmax_step(vecs, bias, users, positive):
    user_f = users.astype(jnp.float32)
    user_square = lax.optimization_barrier(jnp.sum(user_f * user_f, -1, keepdims=True))
    inverse = lax.rsqrt(user_square + 1e-06)
    unit = user_f * inverse
    unit_b = unit.astype(jnp.bfloat16)
    logits = logit_scale * lax.dot_general(unit_b, vecs, (((1,), (1,)), ((), ())), preferred_element_type=jnp.float32) - bias.astype(jnp.float32)[None, :]
    exponent = jnp.exp(logits)
    denominator = lax.optimization_barrier(jnp.sum(exponent, 1))
    picked = jnp.take_along_axis(logits, positive[:, None], 1)[:, 0]
    loss = jnp.log(denominator) - picked
    onehot = (jnp.arange(logits.shape[1], dtype=jnp.int32)[None, :] == positive[:, None]).astype(jnp.float32)
    residue = (exponent / denominator[:, None] - onehot).astype(jnp.bfloat16)
    direction = logit_scale * jnp.dot(residue, vecs, preferred_element_type=jnp.float32)
    user_grad = inverse * (direction - lax.optimization_barrier(jnp.sum(direction * unit, -1, keepdims=True)) * unit)
    item_grad = logit_scale * lax.dot_general(residue, unit_b, (((0,), (0,)), ((), ())), preferred_element_type=jnp.float32)
    return (loss, user_grad, item_grad)

def reference(item_feats, owner, id_row, counts, occurrence, users, w_first, w_second, id_table):
    group_items = N_BLK * U_DEV
    group_rows = N_BLK * B_DEV
    feats_g = item_feats.reshape(N_SHARD, group_items, F)
    index_g = (owner[:, 0] * TAB_DEV + id_row).astype(jnp.int32).reshape(N_SHARD, group_items)
    counts_g = counts.reshape(N_SHARD, group_items)
    occur_g = occurrence.reshape(N_SHARD, group_rows)
    users_g = users.reshape(N_SHARD, group_rows, E)

    def one_group(pieces):
        feats, index, count, occur, user_rows = pieces
        vecs = encode_items(feats, id_table[index], w_first, w_second)
        bias = jnp.log(count.astype(jnp.float32)).astype(jnp.bfloat16)
        positive = (jnp.arange(group_rows, dtype=jnp.int32) // B_DEV * U_DEV + occur).astype(jnp.int32)
        return softmax_step(vecs, bias, user_rows, positive)
    loss, user_grad, item_grad = lax.map(one_group, (feats_g, index_g, counts_g, occur_g, users_g))
    return (loss.reshape(USERS), user_grad.reshape(USERS, E), item_grad.reshape(UNIQ, E))
```

```python
import functools

import jax
import jax.numpy as jnp
from jax import lax
from jax.experimental import pallas as pl
from jax.experimental.pallas import tpu as pltpu
from jax.sharding import PartitionSpec as P

logit_scale = 48.0
log2_e = 1.4426950408889634
exponent_scale = logit_scale * log2_e
vmem = pl.BlockSpec(memory_space=pltpu.VMEM)
f32, bf16 = jnp.float32, jnp.bfloat16


def call(kernel, out_shape, flops, moved, exps=0):
    many = isinstance(out_shape, (tuple, list))
    return pl.pallas_call(
        kernel,
        out_shape=out_shape,
        out_specs=[vmem] * len(out_shape) if many else vmem,
        compiler_params=pltpu.CompilerParams(vmem_limit_bytes=48 * 2**20),
        cost_estimate=pl.CostEstimate(flops=flops, bytes_accessed=moved, transcendentals=exps),
    )


def dot(a, b, contract=((1,), (0,))):
    return lax.dot_general(a, b, (contract, ((), ())), preferred_element_type=f32)


def iota(shape, dim):
    return lax.broadcasted_iota(jnp.int32, shape, dim)


def place_kernel(owners, capacity, owner_ref, id_ref, ids_ref, placing_ref):
    n = owner_ref.shape[1]
    eye = iota((n, n), 0) == iota((n, n), 1)
    owner = jnp.sum(jnp.where(eye, owner_ref[...], 0).astype(f32), 1, keepdims=True)
    ids = jnp.sum(jnp.where(eye, id_ref[...], 0).astype(f32), 1, keepdims=True)
    hot = jnp.where(owner == iota((n, owners), 1).astype(f32), 1.0, 0.0)
    earlier = jnp.where(iota((n, n), 0) > iota((n, n), 1), 1.0, 0.0).astype(bf16)
    before = dot(earlier, hot.astype(bf16))
    rank = jnp.sum(before * hot, 1, keepdims=True)
    high = jnp.floor(ids * (1.0 / 32.0))
    low = ids - 32.0 * high
    lane = iota((n, 128), 1).astype(f32)
    parts = jnp.where(lane == rank, high, 0.0) + jnp.where(lane == rank + capacity, low, 0.0)
    ids_ref[...] = dot(hot.astype(bf16), parts.astype(bf16), ((0,), (0,))).astype(jnp.int32)
    position = owner * capacity + rank
    placing_ref[...] = jnp.where(
        position == iota((n, owners * capacity), 1).astype(f32), 1.0, 0.0
    ).astype(bf16)


def rows_kernel(capacity, ids_ref, table_ref, out_ref):
    peers = ids_ref.shape[0]
    slots = peers * capacity
    peer_of = iota((slots, peers), 0) // capacity
    spread = jnp.where(peer_of == iota((slots, peers), 1), 1.0, 0.0).astype(bf16)
    parts = dot(spread, ids_ref[...].astype(bf16))
    lane, slot = iota((slots, 128), 1), iota((slots, 128), 0) % capacity
    weight = jnp.where(lane == slot, 32.0, 0.0) + jnp.where(lane == slot + capacity, 1.0, 0.0)
    ids = jnp.sum(parts * weight, 1, keepdims=True)
    hot = jnp.where(ids == iota((slots, table_ref.shape[0]), 1).astype(f32), 1.0, 0.0)
    out_ref[...] = dot(hot.astype(bf16), table_ref[...]).astype(bf16)


def encode_kernel(pre_ref, placing_ref, rows_ref, second_ref, out_ref):
    rows = dot(placing_ref[...], rows_ref[...])
    hidden = jnp.maximum(pre_ref[...] + rows, 0.0).astype(bf16)
    emb = dot(hidden, second_ref[...])
    square = jnp.sum(emb * emb, -1, keepdims=True)
    out_ref[...] = (emb * lax.rsqrt(square + 1e-06)).astype(bf16)


def partial_kernel(vecs_ref, bias_ref, units_ref, out_ref):
    blocks, rows = out_ref.shape
    peers, n, width = vecs_ref.shape

    def step(t, carry):
        units = units_ref[pl.ds(2 * t, 2), :rows, :].reshape(2 * rows, width)
        total = jnp.zeros((8, 2 * rows), f32)
        for i in range(peers // 2):
            vecs = vecs_ref[2 * i : 2 * i + 2].reshape(2 * n, width)
            logits = dot(vecs, units, ((1,), (1,)))
            bias = bias_ref[2 * i : 2 * i + 2].reshape(2 * n, 128)
            bias = jnp.concatenate([bias] * (2 * rows // 128), 1)
            total += jnp.sum(jnp.exp2(logits * exponent_scale - bias).reshape(-1, 8, 2 * rows), 0)
        total = jnp.sum(total, 0, keepdims=True)
        out_ref[pl.ds(2 * t, 1), :] = total[:, :rows]
        out_ref[pl.ds(2 * t + 1, 1), :] = total[:, rows:]
        return carry

    lax.fori_loop(0, blocks // 2, step, 0)


def user_kernel(
    place_ref, mine_ref, other_ref, bias_ref, unit_b_ref, users_ref, occurrence_ref, loss_ref, grad_ref, exps
):
    peers, n, width = mine_ref.shape
    rows = users_ref.shape[0]
    unit_b = unit_b_ref[...]
    total = jnp.zeros((rows, 128), f32)
    for half, ref in enumerate((mine_ref, other_ref)):
        for i in range(peers):
            logits = dot(unit_b, ref[i], ((1,), (1,))) * exponent_scale - bias_ref[half, i : i + 1, :]
            exponent = jnp.exp2(logits)
            total += exponent
            exps[:, (half * peers + i) * n : (half * peers + i + 1) * n] = exponent
    denominator = jnp.sum(total, 1, keepdims=True)
    place = place_ref[0]
    eye = iota((rows, rows), 0) == iota((rows, rows), 1)
    occurrence = jnp.sum(jnp.where(eye, occurrence_ref[...], 0).astype(f32), 1, keepdims=True)
    hot = jnp.where(occurrence == iota((rows, n), 1).astype(f32), 1.0, 0.0)
    own = pl.ds(pl.multiple_of(place * n, n), n)
    own_logits = dot(unit_b, mine_ref[place], ((1,), (1,))) * exponent_scale
    own_logits = own_logits - bias_ref[0, pl.ds(place, 1), :]
    picked = jnp.sum(own_logits * hot, 1, keepdims=True) * (1.0 / log2_e)
    loss = jnp.log(denominator) - picked
    loss_ref[...] = jnp.sum(jnp.where(eye, loss, 0.0), 0, keepdims=True)
    exps[:, own] = exps[:, own] - hot * denominator
    inverse = 1.0 / denominator
    direction = jnp.zeros((rows, width), f32)
    for half, ref in enumerate((mine_ref, other_ref)):
        for i in range(peers // 2):
            start = (half * peers + 2 * i) * n
            residue = (exps[:, start : start + 2 * n] * inverse).astype(bf16)
            direction += dot(residue, ref[2 * i : 2 * i + 2].reshape(2 * n, width))
    direction = logit_scale * direction
    user_f = users_ref[...].astype(f32)
    scale = lax.rsqrt(jnp.sum(user_f * user_f, -1, keepdims=True) + 1e-06)
    unit = user_f * scale
    grad_ref[...] = scale * (direction - jnp.sum(direction * unit, -1, keepdims=True) * unit)


def item_kernel(block_ref, vecs_ref, bias_ref, units_ref, first_ref, second_ref, occurrence_ref, out_ref):
    n, width = vecs_ref.shape
    blocks, rows = first_ref.shape
    vecs = vecs_ref[...]
    bias = jnp.concatenate([bias_ref[...]] * (rows // 128), 1)
    block = block_ref[0]
    grad = jnp.zeros((n, width), f32)
    for b in range(blocks):
        units = units_ref[b, :rows, :]
        inverse = 1.0 / (first_ref[b : b + 1, :] + second_ref[b : b + 1, :])
        exponent = jnp.exp2(dot(vecs, units, ((1,), (1,))) * exponent_scale - bias)
        occurrence = jnp.where(block == b, occurrence_ref[...], -1)
        hot = jnp.where(occurrence == iota((n, rows), 0), 1.0, 0.0)
        residue = (exponent * inverse - hot).astype(bf16)
        grad += dot(residue, units)
    out_ref[...] = logit_scale * grad


def shards(item_feats, owner, id_row, counts, occurrence, users, w_first, w_second, id_table):
    n, width = item_feats.shape[0], users.shape[1]
    rows = users.shape[0]
    owners, blocks = lax.axis_size("shard"), lax.axis_size("blk")
    capacity = 2 * n // owners
    slots = owners * capacity
    peers = blocks // 2
    block = lax.axis_index("blk")
    core, place = block % 2, block // 2
    swap = [(i, i ^ 1) for i in range(blocks)]

    ids, placing = call(
        functools.partial(place_kernel, owners, capacity),
        (
            jax.ShapeDtypeStruct((owners, 128), jnp.int32),
            jax.ShapeDtypeStruct((n, slots), bf16),
        ),
        8 * n * n * owners,
        4 * owners * 128,
    )(owner.reshape(1, n), id_row.reshape(1, n))
    ids = lax.all_to_all(ids.reshape(owners, 1, 128), "shard", 0, 0, tiled=True)

    user_f = users.astype(f32)
    unit_b = (user_f * lax.rsqrt(jnp.sum(user_f * user_f, -1, keepdims=True) + 1e-06)).astype(bf16)
    bias = jnp.log(counts.astype(f32)).astype(bf16)
    extra = jnp.pad(bias[None, :], ((0, 15), (0, width - n)))
    units = lax.all_gather(jnp.concatenate([unit_b, extra]), "blk", axis=0, tiled=False)
    biases = units[:, rows, :n].astype(f32) * log2_e
    biases = jnp.roll(biases.reshape(peers, 2, n).transpose(1, 0, 2), core, 0)
    bias_columns = jnp.broadcast_to(biases[0][:, :, None], (peers, n, 128))
    own_bias = lax.dynamic_index_in_dim(bias_columns, place, 0, False)

    table_rows = call(
        functools.partial(rows_kernel, capacity),
        jax.ShapeDtypeStruct((slots, id_table.shape[1]), bf16),
        2 * slots * id_table.size,
        2 * id_table.size,
    )(ids.reshape(owners, 128), id_table)
    received = lax.all_to_all(
        table_rows.reshape(owners, capacity, -1), "shard", 0, 0, tiled=True
    ).reshape(slots, -1)
    pre = jnp.dot(item_feats, w_first, preferred_element_type=f32)
    vecs = call(
        encode_kernel,
        jax.ShapeDtypeStruct((n, width), bf16),
        2 * n * slots * w_first.shape[1],
        2 * received.size,
    )(pre, placing, received, w_second)

    mine = lax.all_to_all(
        jnp.broadcast_to(vecs[None], (peers, n, width)),
        "blk",
        0,
        0,
        axis_index_groups=[list(range(c, blocks, 2)) for c in range(2)],
        tiled=True,
    )
    other = lax.ppermute(mine, "blk", swap)
    first = call(
        partial_kernel,
        jax.ShapeDtypeStruct((blocks, rows), f32),
        2 * blocks * rows * peers * n * width,
        units.size * 2,
        blocks * rows * peers * n,
    )(mine, bias_columns, units)
    second = lax.ppermute(first, "blk", swap)
    smem = pl.BlockSpec(memory_space=pltpu.SMEM)
    params = pltpu.CompilerParams(vmem_limit_bytes=48 * 2**20)
    loss, user_grad = pl.pallas_call(
        user_kernel,
        out_shape=(jax.ShapeDtypeStruct((1, rows), f32), jax.ShapeDtypeStruct((rows, width), f32)),
        in_specs=[smem] + [vmem] * 6,
        out_specs=[vmem] * 2,
        scratch_shapes=[pltpu.VMEM((rows, blocks * n), f32)],
        compiler_params=params,
        cost_estimate=pl.CostEstimate(
            flops=4 * rows * blocks * n * width,
            bytes_accessed=2 * units.size,
            transcendentals=rows * blocks * n,
        ),
    )(place[None], mine, other, biases, unit_b, users, occurrence.reshape(1, rows))
    item_grad = pl.pallas_call(
        item_kernel,
        out_shape=jax.ShapeDtypeStruct((n, width), f32),
        in_specs=[smem] + [vmem] * 6,
        out_specs=vmem,
        compiler_params=params,
        cost_estimate=pl.CostEstimate(
            flops=4 * rows * blocks * n * width,
            bytes_accessed=2 * units.size,
            transcendentals=rows * blocks * n,
        ),
    )(block[None], vecs, own_bias, units, first, second, occurrence.reshape(1, rows))
    return (loss.reshape(rows), user_grad, item_grad)


def solution(mesh):
    return jax.shard_map(
        shards,
        mesh=mesh,
        in_specs=(
            P(("shard", "blk"), None),
            P(("shard", "blk"), None),
            P(("shard", "blk")),
            P(("shard", "blk")),
            P(("shard", "blk")),
            P(("shard", "blk"), None),
            P(),
            P(),
            P("shard", None),
        ),
        out_specs=(P(("shard", "blk")), P(("shard", "blk"), None), P(("shard", "blk"), None)),
        check_vma=False,
    )
```

```python
import functools

import jax
import jax.numpy as jnp
from jax import lax
from jax.experimental import pallas as pl
from jax.experimental.pallas import tpu as pltpu
from jax.sharding import PartitionSpec as P

logit_scale = 48.0
log2_e = 1.4426950408889634
exponent_scale = logit_scale * log2_e
vmem = pl.BlockSpec(memory_space=pltpu.VMEM)
far_memory = pl.BlockSpec(memory_space=pltpu.HBM)
f32, bf16 = jnp.float32, jnp.bfloat16


def call(kernel, out_shape, flops, moved, exps=0, in_specs=None, scratch=(), room=16):
    options = {} if in_specs is None else {"in_specs": in_specs}
    return pl.pallas_call(
        kernel,
        out_shape=out_shape,
        out_specs=[vmem] * len(out_shape) if isinstance(out_shape, tuple) else vmem,
        scratch_shapes=scratch,
        compiler_params=pltpu.CompilerParams(vmem_limit_bytes=room * 2**20),
        cost_estimate=pl.CostEstimate(flops=flops, bytes_accessed=moved, transcendentals=exps),
        **options,
    )


def dot(a, b, contract=((1,), (0,))):
    return lax.dot_general(a, b, (contract, ((), ())), preferred_element_type=f32)


def iota(shape, dim):
    return lax.broadcasted_iota(jnp.int32, shape, dim)


def place_kernel(
    owners,
    capacity,
    owner_in,
    id_in,
    users_in,
    counts_in,
    ids_ref,
    placing_ref,
    payload_ref,
    owner_ref,
    id_ref,
    users_ref,
    counts_ref,
    sems,
):
    pairs = (owner_in, owner_ref), (id_in, id_ref), (users_in, users_ref), (counts_in, counts_ref)
    copies = [pltpu.make_async_copy(*pair, sems.at[i]) for i, pair in enumerate(pairs)]
    for copy in copies:
        copy.start()
    for copy in copies:
        copy.wait()
    n = owner_ref.shape[1]
    eye = iota((n, n), 0) == iota((n, n), 1)
    owner = jnp.sum(jnp.where(eye, owner_ref[...], 0).astype(f32), 1, keepdims=True)
    ids = jnp.sum(jnp.where(eye, id_ref[...], 0).astype(f32), 1, keepdims=True)
    hot = jnp.where(owner == iota((n, owners), 1).astype(f32), 1.0, 0.0)
    earlier = jnp.where(iota((n, n), 0) > iota((n, n), 1), 1.0, 0.0).astype(bf16)
    before = dot(earlier, hot.astype(bf16))
    rank = jnp.sum(before * hot, 1, keepdims=True)
    high = jnp.floor(ids * (1.0 / 32.0))
    low = ids - 32.0 * high
    lane = iota((n, 128), 1).astype(f32)
    parts = jnp.where(lane == rank, high, 0.0) + jnp.where(lane == rank + capacity, low, 0.0)
    ids_ref[...] = dot(hot.astype(bf16), parts.astype(bf16), ((0,), (0,))).astype(jnp.int32)
    position = owner * capacity + rank
    placing_ref[...] = jnp.where(
        position == iota((n, owners * capacity), 1).astype(f32), 1.0, 0.0
    ).astype(bf16)
    rows = users_ref.shape[0]
    user_f = users_ref[...].astype(f32)
    inverse = lax.rsqrt(jnp.sum(user_f * user_f, -1, keepdims=True) + 1e-06)
    payload_ref[:rows, :] = (user_f * inverse).astype(bf16)
    bias = jnp.broadcast_to(jnp.log(counts_ref[...].astype(f32)), (16, n))
    payload_ref[rows:, :] = jnp.concatenate([bias] * (payload_ref.shape[1] // n), 1).astype(bf16)


def table_kernel(table_in, after_ref, table_ref, sem):
    copy = pltpu.make_async_copy(table_in, table_ref, sem)
    copy.start()
    copy.wait()


def rows_kernel(capacity, ids_ref, table_ref, out_ref):
    peers = ids_ref.shape[0]
    slots = peers * capacity
    peer_of = iota((slots, peers), 0) // capacity
    spread = jnp.where(peer_of == iota((slots, peers), 1), 1.0, 0.0).astype(bf16)
    parts = dot(spread, ids_ref[...].astype(bf16))
    lane, slot = iota((slots, 128), 1), iota((slots, 128), 0) % capacity
    weight = jnp.where(lane == slot, 32.0, 0.0) + jnp.where(lane == slot + capacity, 1.0, 0.0)
    ids = jnp.sum(parts * weight, 1, keepdims=True)
    hot = jnp.where(ids == iota((slots, table_ref.shape[0]), 1).astype(f32), 1.0, 0.0).astype(bf16)
    out_ref[...] = dot(hot, table_ref[...]).astype(bf16).reshape(out_ref.shape)


def encode_kernel(pre_ref, placing_ref, rows_ref, second_ref, out_ref):
    rows = dot(placing_ref[...], rows_ref[...].reshape(placing_ref.shape[1], -1))
    hidden = jnp.maximum(pre_ref[...] + rows, 0.0).astype(bf16)
    emb = dot(hidden, second_ref[...])
    square = jnp.sum(emb * emb, -1, keepdims=True)
    vecs = (emb * lax.rsqrt(square + 1e-06)).astype(bf16)
    for i in range(out_ref.shape[0]):
        out_ref[i] = vecs


def column(row):
    n = row.shape[1]
    return jnp.sum(jnp.where(iota((n, n), 0) == iota((n, n), 1), row, 0.0), 1, keepdims=True)


def sums(place, vecs_ref, bias_ref, unit_refs, store):
    peers, n, width = vecs_ref.shape
    rows = unit_refs[0].shape[1] - 16
    biases = [bias_ref[pl.ds(lax.rem(place - i + peers, peers), 1), :] for i in range(peers)]
    biases = [jnp.broadcast_to(column(bias), (n, 128)) for bias in biases]
    for t in range(0, 2 * len(unit_refs), 2):
        units = unit_refs[t // 2][:, :rows, :].reshape(2 * rows, width)

        def step(i, total):
            vecs = vecs_ref[pl.ds(2 * i, 2)].reshape(2 * n, width)
            logits = dot(vecs, units, ((1,), (1,)))
            bias = jnp.concatenate(biases[2 * i : 2 * i + 2])
            bias = jnp.concatenate([bias] * (2 * rows // 128), 1)
            exponent = jnp.exp2(logits * exponent_scale - bias)
            return total + jnp.sum(exponent.reshape(-1, 8, 2 * rows), 0)

        total = jnp.zeros((8, 2 * rows), f32)
        for i in range(peers // 2):
            total = step(i, total)
        total = jnp.sum(total, 0, keepdims=True)
        store(t, total[:, :rows])
        store(t + 1, total[:, rows:])


def first_kernel(place_ref, vecs_ref, bias_ref, *refs):
    out_ref = refs[-1]

    def store(t, value):
        out_ref[t : t + 1, :] = value

    sums(place_ref[0], vecs_ref, bias_ref, refs[:-1], store)


def item_sum(vecs, bias, units, sums_ref, hot):
    n, width = vecs.shape
    bias = jnp.broadcast_to(column(bias), (n, 128))
    grad = jnp.zeros((n, width), f32)
    rows = units[0].shape[1] - 16
    for t in range(2 * len(units)):
        unit = units[t // 2][t % 2, :rows, :]
        exponent = jnp.exp2(
            dot(vecs, unit, ((1,), (1,))) * exponent_scale
            - jnp.concatenate([bias] * (rows // 128), 1)
        )
        residue = exponent * (1.0 / sums_ref[t : t + 1, :])
        if t == 0 and hot is not None:
            residue = residue - hot
        grad += dot(residue.astype(bf16), unit)
    return logit_scale * grad


def second_kernel(place_ref, vecs_ref, bias_ref, first_ref, *refs):
    units, sums_ref, grad_ref = refs[:-2], refs[-2], refs[-1]
    place = place_ref[0]

    def store(t, value):
        sums_ref[t : t + 1, :] = first_ref[t : t + 1, :] + value

    sums(place, vecs_ref, bias_ref, units, store)
    grad_ref[...] = item_sum(vecs_ref[place], bias_ref[0:1, :], units, sums_ref, None)


def user_kernel(
    place_ref,
    mine_ref,
    other_ref,
    bias_ref,
    other_bias_ref,
    sums_ref,
    users_ref,
    occurrence_ref,
    units_ref,
    loss_ref,
    grad_ref,
    exps,
):
    peers, n, width = mine_ref.shape
    rows = users_ref.shape[0]
    place = place_ref[0]
    unit_b = units_ref[0, :rows, :]
    denominator = column(sums_ref[0:1, :])
    inverse = 1.0 / denominator
    occurrence = column(occurrence_ref[...].astype(f32))
    hot = jnp.where(occurrence == iota((rows, n), 1).astype(f32), 1.0, 0.0)
    direction = jnp.zeros((rows, width), f32)
    for half, (ref, bias_half) in enumerate(((mine_ref, bias_ref), (other_ref, other_bias_ref))):
        for i in range(peers):
            bias = bias_half[pl.ds(lax.rem(place - i + peers, peers), 1), :]
            logits = dot(unit_b, ref[i], ((1,), (1,))) * exponent_scale - bias
            exps[:, i * n : (i + 1) * n] = jnp.exp2(logits) * inverse
        if half == 0:
            own = pl.ds(pl.multiple_of(place * n, n), n)
            exps[:, own] = exps[:, own] - hot
        direction += dot(exps[...].astype(bf16), ref[...].reshape(peers * n, width))
    own_logits = dot(unit_b, mine_ref[place], ((1,), (1,))) * exponent_scale - bias_ref[0:1, :]
    picked = jnp.sum(own_logits * hot, 1, keepdims=True) * (1.0 / log2_e)
    loss = jnp.log(denominator) - picked
    eye = iota((rows, rows), 0) == iota((rows, rows), 1)
    loss_ref[...] = jnp.sum(jnp.where(eye, loss, 0.0), 0, keepdims=True)
    direction = logit_scale * direction
    user_f = users_ref[...].astype(f32)
    scale = lax.rsqrt(jnp.sum(user_f * user_f, -1, keepdims=True) + 1e-06)
    unit = user_f * scale
    grad_ref[...] = scale * (direction - jnp.sum(direction * unit, -1, keepdims=True) * unit)


def item_kernel(place_ref, mine_ref, bias_ref, sums_ref, occurrence_ref, taken_ref, *refs):
    units, out_ref = refs[:-1], refs[-1]
    n, rows = mine_ref.shape[1], occurrence_ref.shape[1]
    hot = jnp.where(occurrence_ref[...] == iota((n, rows), 0), 1.0, 0.0)
    grad = item_sum(mine_ref[place_ref[0]], bias_ref[0:1, :], units, sums_ref, hot)
    out_ref[...] = grad + taken_ref[...]


def shards(item_feats, owner, id_row, counts, occurrence, users, w_first, w_second, id_table):
    n, width = item_feats.shape[0], users.shape[1]
    rows = users.shape[0]
    owners, blocks = lax.axis_size("shard"), lax.axis_size("blk")
    capacity = 2 * n // owners
    slots = owners * capacity
    peers = blocks // 2
    block = lax.axis_index("blk")
    core, place = block % 2, block // 2
    swap = [(i, i ^ 1) for i in range(blocks)]

    shape = jax.ShapeDtypeStruct
    place_sizes = (
        shape((owners, 128), jnp.int32),
        shape((n, slots), bf16),
        shape((rows + 16, width), bf16),
    )
    ids_sent, placing, payload = call(
        functools.partial(place_kernel, owners, capacity),
        place_sizes,
        8 * n * n * owners,
        4 * owners * 128,
        in_specs=[far_memory] * 4,
        scratch=[
            pltpu.VMEM((1, n), jnp.int32),
            pltpu.VMEM((1, n), jnp.int32),
            pltpu.VMEM((rows, width), bf16),
            pltpu.VMEM((1, n), jnp.int32),
            pltpu.SemaphoreType.DMA((4,)),
        ],
        room=60,
    )(owner.reshape(1, n), id_row.reshape(1, n), users, counts.reshape(1, n))
    ids = lax.all_to_all(ids_sent.reshape(owners, 1, 128), "shard", 0, 0, tiled=True)
    table = call(
        table_kernel,
        shape(id_table.shape, bf16),
        0,
        4 * id_table.size,
        in_specs=[far_memory] * 2,
        scratch=[pltpu.SemaphoreType.DMA],
    )(id_table, ids_sent)

    def turn(array, step, other_step=None):
        steps = (step, step if other_step is None else other_step)
        pairs = [(i, (i + 2 * steps[i % 2]) % blocks) for i in range(blocks)]
        return lax.ppermute(array, "blk", pairs)

    table_rows = call(
        functools.partial(rows_kernel, capacity),
        shape((owners, capacity, id_table.shape[1]), bf16),
        2 * slots * id_table.size,
        2 * id_table.size,
    )(ids.reshape(owners, 128), table)
    far = turn(payload, peers // 2)
    table_rows, payload, far = lax.optimization_barrier((table_rows, payload, far))
    received = lax.all_to_all(table_rows, "shard", 0, 0, tiled=True)
    pair = jnp.stack([payload, far])
    units = [pair, turn(pair, 1), turn(pair, -1), turn(pair, 2, -2)]
    bias = [u[i, rows : rows + 1, :n] for u in units for i in range(2)]
    first_core = core == 0
    bias_2, bias_6 = jnp.where(first_core, bias[6], bias[7]), jnp.where(first_core, bias[7], bias[6])
    ordered = [bias[0], bias[2], bias_2, bias[5], bias[1], bias[3], bias_6, bias[4]]
    biases = jnp.concatenate(ordered).astype(f32) * log2_e
    other_biases = lax.ppermute(biases, "blk", swap)

    pre = jnp.dot(item_feats, w_first, preferred_element_type=f32)
    vecs = call(
        encode_kernel,
        shape((peers, n, width), bf16),
        2 * n * slots * w_first.shape[1],
        2 * received.size,
    )(pre, placing, received, w_second)

    mine = lax.all_to_all(
        vecs,
        "blk",
        0,
        0,
        axis_index_groups=[list(range(c, blocks, 2)) for c in range(2)],
        tiled=True,
    )
    mine, biases, other_biases = lax.optimization_barrier((mine, biases, other_biases))
    other = lax.ppermute(mine, "blk", swap)
    smem = pl.BlockSpec(memory_space=pltpu.SMEM)

    def step(kernel, out_shape, pairs, inputs, scratch=()):
        specs = [smem] + [vmem] * (len(inputs) - 1)
        moved = peers * rows * width * 4
        return call(kernel, out_shape, 2 * pairs * width, moved, pairs, specs, scratch, 48)(*inputs)

    at, occurrence = place[None], occurrence.reshape(1, rows)
    pairs = peers * rows * peers * n
    first = step(first_kernel, shape((peers, rows), f32), pairs, (at, mine, biases, *units))
    total, given = step(
        second_kernel,
        (shape((peers, rows), f32), shape((n, width), f32)),
        pairs,
        (at, other, other_biases, first, *units),
    )
    taken = lax.ppermute(given, "blk", swap)
    loss, user_grad = step(
        user_kernel,
        (shape((1, rows), f32), shape((rows, width), f32)),
        pairs,
        (at, mine, other, biases, other_biases, total, users, occurrence, pair),
        [pltpu.VMEM((rows, peers * n), f32)],
    )
    item_grad = step(
        item_kernel,
        shape((n, width), f32),
        peers * rows * n,
        (at, mine, biases, total, occurrence, taken, *units),
    )
    return (loss.reshape(rows), user_grad, item_grad)


def solution(mesh):
    return jax.shard_map(
        shards,
        mesh=mesh,
        in_specs=(
            P(("shard", "blk"), None),
            P(("shard", "blk"), None),
            P(("shard", "blk")),
            P(("shard", "blk")),
            P(("shard", "blk")),
            P(("shard", "blk"), None),
            P(),
            P(),
            P("shard", None),
        ),
        out_specs=(P(("shard", "blk")), P(("shard", "blk"), None), P(("shard", "blk"), None)),
        check_vma=False,
    )
```

```python
import functools

import jax
import jax.numpy as jnp
from jax import lax
from jax.experimental import pallas as pl
from jax.experimental.pallas import tpu as pltpu
from jax.sharding import PartitionSpec as P

logit_scale = 48.0
log2_e = 1.4426950408889634
exponent_scale = logit_scale * log2_e
vmem = pl.BlockSpec(memory_space=pltpu.VMEM)
far_memory = pl.BlockSpec(memory_space=pltpu.HBM)
f32, bf16 = jnp.float32, jnp.bfloat16


def call(kernel, out_shape, flops, moved, exps=0, in_specs=None, scratch=(), room=16):
    options = {} if in_specs is None else {"in_specs": in_specs}
    return pl.pallas_call(
        kernel,
        out_shape=out_shape,
        out_specs=[vmem] * len(out_shape) if isinstance(out_shape, tuple) else vmem,
        scratch_shapes=scratch,
        compiler_params=pltpu.CompilerParams(vmem_limit_bytes=room * 2**20),
        cost_estimate=pl.CostEstimate(flops=flops, bytes_accessed=moved, transcendentals=exps),
        **options,
    )


def dot(a, b, contract=((1,), (0,))):
    return lax.dot_general(a, b, (contract, ((), ())), preferred_element_type=f32)


def iota(shape, dim):
    return lax.broadcasted_iota(jnp.int32, shape, dim)


def place_kernel(
    owners,
    capacity,
    owner_in,
    id_in,
    users_in,
    ids_ref,
    placing_ref,
    payload_ref,
    owner_ref,
    id_ref,
    users_ref,
    sems,
):
    pairs = (owner_in, owner_ref), (id_in, id_ref), (users_in, users_ref)
    copies = [pltpu.make_async_copy(*pair, sems.at[i]) for i, pair in enumerate(pairs)]
    for copy in copies:
        copy.start()
    for copy in copies:
        copy.wait()
    n = owner_ref.shape[1]
    eye = iota((n, n), 0) == iota((n, n), 1)
    owner = jnp.sum(jnp.where(eye, owner_ref[...], 0).astype(f32), 1, keepdims=True)
    ids = jnp.sum(jnp.where(eye, id_ref[...], 0).astype(f32), 1, keepdims=True)
    hot = jnp.where(owner == iota((n, owners), 1).astype(f32), 1.0, 0.0)
    earlier = jnp.where(iota((n, n), 0) > iota((n, n), 1), 1.0, 0.0).astype(bf16)
    before = dot(earlier, hot.astype(bf16))
    rank = jnp.sum(before * hot, 1, keepdims=True)
    high = jnp.floor(ids * (1.0 / 32.0))
    low = ids - 32.0 * high
    lane = iota((n, 128), 1).astype(f32)
    parts = jnp.where(lane == rank, high, 0.0) + jnp.where(lane == rank + capacity, low, 0.0)
    ids_ref[...] = dot(hot.astype(bf16), parts.astype(bf16), ((0,), (0,))).astype(jnp.int32)
    position = owner * capacity + rank
    placing_ref[...] = jnp.where(
        position == iota((n, owners * capacity), 1).astype(f32), 1.0, 0.0
    ).astype(bf16)
    user_f = users_ref[...].astype(f32)
    inverse = lax.rsqrt(jnp.sum(user_f * user_f, -1, keepdims=True) + 1e-06)
    payload_ref[...] = (user_f * inverse).astype(bf16)


def table_kernel(table_in, table_ref, sem):
    copy = pltpu.make_async_copy(table_in, table_ref, sem)
    copy.start()
    copy.wait()


def pair_kernel(near_ref, far_ref, out_ref):
    out_ref[0] = near_ref[...]
    out_ref[1] = far_ref[...]


def ready_kernel(one_ref, two_ref, three_ref, out_ref):
    out_ref[...] = jnp.zeros_like(out_ref)


def rows_kernel(capacity, ids_ref, table_ref, out_ref):
    peers = ids_ref.shape[0]
    slots = peers * capacity
    peer_of = iota((slots, peers), 0) // capacity
    spread = jnp.where(peer_of == iota((slots, peers), 1), 1.0, 0.0).astype(bf16)
    parts = dot(spread, ids_ref[...].astype(bf16))
    lane, slot = iota((slots, 128), 1), iota((slots, 128), 0) % capacity
    weight = jnp.where(lane == slot, 32.0, 0.0) + jnp.where(lane == slot + capacity, 1.0, 0.0)
    ids = jnp.sum(parts * weight, 1, keepdims=True)
    hot = jnp.where(ids == iota((slots, table_ref.shape[0]), 1).astype(f32), 1.0, 0.0).astype(bf16)
    out_ref[...] = dot(hot, table_ref[...]).astype(bf16).reshape(out_ref.shape)


def encode_kernel(pre_ref, placing_ref, rows_ref, second_ref, counts_ref, out_ref):
    rows = dot(placing_ref[...], rows_ref[...].reshape(placing_ref.shape[1], -1))
    hidden = jnp.maximum(pre_ref[...] + rows, 0.0).astype(bf16)
    emb = dot(hidden, second_ref[...])
    square = jnp.sum(emb * emb, -1, keepdims=True)
    vecs = (emb * lax.rsqrt(square + 1e-06)).astype(bf16)
    n, width = vecs.shape
    bias = jnp.broadcast_to(jnp.log(counts_ref[...].astype(f32)), (16, n))
    bias = jnp.concatenate([bias] * (width // n), 1).astype(bf16)
    for i in range(out_ref.shape[0]):
        out_ref[i, :n, :] = vecs
        out_ref[i, n:, :] = bias


def bias_row(ref, i, n):
    return ref[i, n : n + 16, :n].astype(f32)[0:1, :] * log2_e


def column(row):
    n = row.shape[1]
    return jnp.sum(jnp.where(iota((n, n), 0) == iota((n, n), 1), row, 0.0), 1, keepdims=True)


def sums(vecs_ref, unit_refs, store):
    peers, width = vecs_ref.shape[0], vecs_ref.shape[2]
    n, rows = vecs_ref.shape[1] - 16, unit_refs[0].shape[1]
    biases = [jnp.broadcast_to(column(bias_row(vecs_ref, i, n)), (n, 128)) for i in range(peers)]
    for t in range(0, 2 * len(unit_refs), 2):
        units = unit_refs[t // 2][...].reshape(2 * rows, width)
        total = jnp.zeros((8, 2 * rows), f32)
        for i in range(0, peers, 2):
            vecs = vecs_ref[i : i + 2, :n, :].reshape(2 * n, width)
            logits = dot(vecs, units, ((1,), (1,)))
            bias = jnp.concatenate([jnp.concatenate(biases[i : i + 2])] * (2 * rows // 128), 1)
            exponent = jnp.exp2(logits * exponent_scale - bias)
            total = total + jnp.sum(exponent.reshape(-1, 8, 2 * rows), 0)
        total = jnp.sum(total, 0, keepdims=True)
        store(t, total[:, :rows])
        store(t + 1, total[:, rows:])


def first_kernel(vecs_ref, ready_ref, *refs):
    out_ref = refs[-1]

    def store(t, value):
        out_ref[t : t + 1, :] = value

    sums(vecs_ref, refs[:-1], store)


def item_sum(place, vecs_ref, units, sums_ref, hot):
    n, width = vecs_ref.shape[1] - 16, vecs_ref.shape[2]
    vecs = vecs_ref[place, :n, :]
    bias = jnp.broadcast_to(column(bias_row(vecs_ref, place, n)), (n, 128))
    grad = jnp.zeros((n, width), f32)
    rows = units[0].shape[1]
    for t in range(2 * len(units)):
        unit = units[t // 2][t % 2]
        exponent = jnp.exp2(
            dot(vecs, unit, ((1,), (1,))) * exponent_scale
            - jnp.concatenate([bias] * (rows // 128), 1)
        )
        residue = exponent * (1.0 / sums_ref[t : t + 1, :])
        if t == 0 and hot is not None:
            residue = residue - hot
        grad += dot(residue.astype(bf16), unit)
    return logit_scale * grad


def second_kernel(place_ref, vecs_ref, first_ref, *refs):
    units, sums_ref, grad_ref = refs[:-2], refs[-2], refs[-1]

    def store(t, value):
        sums_ref[t : t + 1, :] = first_ref[t : t + 1, :] + value

    sums(vecs_ref, units, store)
    grad_ref[...] = item_sum(place_ref[0], vecs_ref, units, sums_ref, None)


def user_kernel(
    place_ref,
    mine_ref,
    other_ref,
    sums_ref,
    users_ref,
    occurrence_ref,
    units_ref,
    loss_ref,
    grad_ref,
    exps,
):
    peers, width = mine_ref.shape[0], mine_ref.shape[2]
    n, rows = mine_ref.shape[1] - 16, users_ref.shape[0]
    place = place_ref[0]
    unit_b = units_ref[0]
    denominator = column(sums_ref[0:1, :])
    inverse = 1.0 / denominator
    occurrence = column(occurrence_ref[...].astype(f32))
    hot = jnp.where(occurrence == iota((rows, n), 1).astype(f32), 1.0, 0.0)
    direction = jnp.zeros((rows, width), f32)
    for half, ref in enumerate((mine_ref, other_ref)):
        for i in range(peers):
            logits = dot(unit_b, ref[i, :n, :], ((1,), (1,))) * exponent_scale
            logits = logits - bias_row(ref, i, n)
            exps[:, i * n : (i + 1) * n] = jnp.exp2(logits) * inverse
        if half == 0:
            own = pl.ds(pl.multiple_of(place * n, n), n)
            exps[:, own] = exps[:, own] - hot
        direction += dot(exps[...].astype(bf16), ref[:, :n, :].reshape(peers * n, width))
    own_logits = dot(unit_b, mine_ref[place, :n, :], ((1,), (1,))) * exponent_scale
    own_logits = own_logits - bias_row(mine_ref, place, n)
    picked = jnp.sum(own_logits * hot, 1, keepdims=True) * (1.0 / log2_e)
    loss = jnp.log(denominator) - picked
    eye = iota((rows, rows), 0) == iota((rows, rows), 1)
    loss_ref[...] = jnp.sum(jnp.where(eye, loss, 0.0), 0, keepdims=True)
    direction = logit_scale * direction
    user_f = users_ref[...].astype(f32)
    scale = lax.rsqrt(jnp.sum(user_f * user_f, -1, keepdims=True) + 1e-06)
    unit = user_f * scale
    grad_ref[...] = scale * (direction - jnp.sum(direction * unit, -1, keepdims=True) * unit)


def item_kernel(place_ref, mine_ref, sums_ref, occurrence_ref, taken_ref, *refs):
    units, out_ref = refs[:-1], refs[-1]
    n, rows = mine_ref.shape[1] - 16, occurrence_ref.shape[1]
    hot = jnp.where(occurrence_ref[...] == iota((n, rows), 0), 1.0, 0.0)
    grad = item_sum(place_ref[0], mine_ref, units, sums_ref, hot)
    out_ref[...] = grad + taken_ref[...]


def shards(item_feats, owner, id_row, counts, occurrence, users, w_first, w_second, id_table):
    n, width = item_feats.shape[0], users.shape[1]
    rows = users.shape[0]
    owners, blocks = lax.axis_size("shard"), lax.axis_size("blk")
    capacity = 2 * n // owners
    slots = owners * capacity
    peers = blocks // 2
    block = lax.axis_index("blk")
    place = block // 2
    swap = [(i, i ^ 1) for i in range(blocks)]

    shape = jax.ShapeDtypeStruct
    long = 10**11
    place_sizes = (
        shape((owners, 128), jnp.int32),
        shape((n, slots), bf16),
        shape((rows, width), bf16),
    )
    ids_sent, placing, payload = call(
        functools.partial(place_kernel, owners, capacity),
        place_sizes,
        8 * n * n * owners,
        4 * owners * 128,
        in_specs=[far_memory] * 3,
        scratch=[
            pltpu.VMEM((1, n), jnp.int32),
            pltpu.VMEM((1, n), jnp.int32),
            pltpu.VMEM((rows, width), bf16),
            pltpu.SemaphoreType.DMA((3,)),
        ],
        room=60,
    )(owner.reshape(1, n), id_row.reshape(1, n), users)
    ids = lax.all_to_all(ids_sent.reshape(owners, 1, 128), "shard", 0, 0, tiled=True)
    table = call(
        table_kernel,
        shape(id_table.shape, bf16),
        long // 20,
        4 * id_table.size,
        in_specs=[far_memory],
        scratch=[pltpu.SemaphoreType.DMA],
    )(id_table)

    def turn(array, step, other_step=None):
        steps = (step, step if other_step is None else other_step)
        pairs = [(i, (i + 2 * steps[i % 2]) % blocks) for i in range(blocks)]
        return lax.ppermute(array, "blk", pairs)

    table_rows = call(
        functools.partial(rows_kernel, capacity),
        shape((owners, capacity, id_table.shape[1]), bf16),
        2 * slots * id_table.size,
        2 * id_table.size,
    )(ids.reshape(owners, 128), table)
    far = turn(payload, peers // 2)
    table_rows, feats = lax.optimization_barrier((table_rows, item_feats))
    pre = jnp.dot(feats, w_first, preferred_element_type=f32)
    received = lax.all_to_all(table_rows, "shard", 0, 0, tiled=True)
    pair = call(pair_kernel, shape((2, rows, width), bf16), long, 4 * rows * width)(payload, far)
    units = [pair, turn(pair, 1), turn(pair, -1), turn(pair, 2, -2)]
    vecs = call(
        encode_kernel,
        shape((peers, n + 16, width), bf16),
        2 * n * slots * w_first.shape[1],
        2 * received.size,
    )(pre, placing, received, w_second, counts.reshape(1, n))

    mine = lax.all_to_all(
        vecs,
        "blk",
        0,
        0,
        axis_index_groups=[list(range(c, blocks, 2)) for c in range(2)],
        tiled=True,
    )
    ready = call(
        ready_kernel, shape((8, 128), f32), long, 1024, in_specs=[pl.BlockSpec(memory_space=pl.ANY)] * 3
    )(*units[1:])
    mine, ready = lax.optimization_barrier((mine, ready))
    other = lax.ppermute(mine, "blk", swap)
    smem = pl.BlockSpec(memory_space=pltpu.SMEM)

    def step(kernel, out_shape, pairs, inputs, scratch=()):
        specs = [smem if i is at else vmem for i in inputs]
        moved = peers * rows * width * 4
        return call(kernel, out_shape, 2 * pairs * width, moved, pairs, specs, scratch, 48)(*inputs)

    at, occurrence = place[None], occurrence.reshape(1, rows)
    pairs = peers * rows * peers * n
    first = step(first_kernel, shape((peers, rows), f32), pairs, (mine, ready, *units))
    total, given = step(
        second_kernel,
        (shape((peers, rows), f32), shape((n, width), f32)),
        pairs,
        (at, other, first, *units),
    )
    taken = lax.ppermute(given, "blk", swap)
    loss, user_grad = step(
        user_kernel,
        (shape((1, rows), f32), shape((rows, width), f32)),
        pairs,
        (at, mine, other, total, users, occurrence, pair),
        [pltpu.VMEM((rows, peers * n), f32)],
    )
    item_grad = step(
        item_kernel,
        shape((n, width), f32),
        peers * rows * n,
        (at, mine, total, occurrence, taken, *units),
    )
    return (loss.reshape(rows), user_grad, item_grad)


def solution(mesh):
    return jax.shard_map(
        shards,
        mesh=mesh,
        in_specs=(
            P(("shard", "blk"), None),
            P(("shard", "blk"), None),
            P(("shard", "blk")),
            P(("shard", "blk")),
            P(("shard", "blk")),
            P(("shard", "blk"), None),
            P(),
            P(),
            P("shard", None),
        ),
        out_specs=(P(("shard", "blk")), P(("shard", "blk"), None), P(("shard", "blk"), None)),
        check_vma=False,
    )
```

```python
import functools

import jax
import jax.numpy as jnp
from jax import lax
from jax.experimental import pallas as pl
from jax.experimental.pallas import tpu as pltpu
from jax.sharding import PartitionSpec as P

logit_scale = 48.0
log2_e = 1.4426950408889634
exponent_scale = logit_scale * log2_e
vmem = pl.BlockSpec(memory_space=pltpu.VMEM)
far_memory = pl.BlockSpec(memory_space=pltpu.HBM)
f32, bf16 = jnp.float32, jnp.bfloat16
extra = 8


def call(kernel, out_shape, flops, moved, exps=0, in_specs=None, scratch=(), room=16, out_specs=None):
    if out_specs is None:
        out_specs = [vmem] * len(out_shape) if isinstance(out_shape, tuple) else vmem
    options = {} if in_specs is None else {"in_specs": in_specs}
    return pl.pallas_call(
        kernel,
        out_shape=out_shape,
        out_specs=out_specs,
        scratch_shapes=scratch,
        compiler_params=pltpu.CompilerParams(vmem_limit_bytes=room * 2**20),
        cost_estimate=pl.CostEstimate(flops=flops, bytes_accessed=moved, transcendentals=exps),
        **options,
    )


def dot(a, b, contract=((1,), (0,))):
    return lax.dot_general(a, b, (contract, ((), ())), preferred_element_type=f32)


def iota(shape, dim):
    return lax.broadcasted_iota(jnp.int32, shape, dim)


def place_kernel(
    owners,
    capacity,
    owner_in,
    id_in,
    users_in,
    ids_ref,
    placing_ref,
    payload_ref,
    owner_ref,
    id_ref,
    users_ref,
    sems,
):
    pairs = (owner_in, owner_ref), (id_in, id_ref), (users_in, users_ref)
    copies = [pltpu.make_async_copy(*pair, sems.at[i]) for i, pair in enumerate(pairs)]
    for copy in copies:
        copy.start()
    for copy in copies:
        copy.wait()
    n = owner_ref.shape[1]
    eye = iota((n, n), 0) == iota((n, n), 1)
    owner = jnp.sum(jnp.where(eye, owner_ref[...], 0).astype(f32), 1, keepdims=True)
    ids = jnp.sum(jnp.where(eye, id_ref[...], 0).astype(f32), 1, keepdims=True)
    hot = jnp.where(owner == iota((n, owners), 1).astype(f32), 1.0, 0.0)
    earlier = jnp.where(iota((n, n), 0) > iota((n, n), 1), 1.0, 0.0).astype(bf16)
    before = dot(earlier, hot.astype(bf16))
    rank = jnp.sum(before * hot, 1, keepdims=True)
    high = jnp.floor(ids * (1.0 / 32.0))
    low = ids - 32.0 * high
    lane = iota((n, 128), 1).astype(f32)
    parts = jnp.where(lane == rank, high, 0.0) + jnp.where(lane == rank + capacity, low, 0.0)
    ids_ref[...] = dot(hot.astype(bf16), parts.astype(bf16), ((0,), (0,))).astype(jnp.int32)
    position = owner * capacity + rank
    placing_ref[...] = jnp.where(
        position == iota((n, owners * capacity), 1).astype(f32), 1.0, 0.0
    ).astype(bf16)
    user_f = users_ref[...].astype(f32)
    inverse = lax.rsqrt(jnp.sum(user_f * user_f, -1, keepdims=True) + 1e-06)
    payload_ref[...] = (user_f * inverse).astype(bf16)


def table_kernel(table_in, table_ref, sem):
    copy = pltpu.make_async_copy(table_in, table_ref, sem)
    copy.start()
    copy.wait()


def pair_kernel(near_ref, far_ref, out_ref):
    out_ref[0] = near_ref[...]
    out_ref[1] = far_ref[...]


def ready_kernel(one_ref, two_ref, three_ref, out_ref):
    out_ref[...] = jnp.zeros_like(out_ref)


def rows_kernel(capacity, ids_ref, table_ref, out_ref, rows_ref, sems):
    peers = ids_ref.shape[0]
    slots = peers * capacity
    peer_of = iota((slots, peers), 0) // capacity
    spread = jnp.where(peer_of == iota((slots, peers), 1), 1.0, 0.0).astype(bf16)
    parts = dot(spread, ids_ref[...].astype(bf16))
    lane, slot = iota((slots, 128), 1), iota((slots, 128), 0) % capacity
    weight = jnp.where(lane == slot, 32.0, 0.0) + jnp.where(lane == slot + capacity, 1.0, 0.0)
    ids = jnp.sum(parts * weight, 1, keepdims=True)
    hot = jnp.where(ids == iota((slots, table_ref.shape[0]), 1).astype(f32), 1.0, 0.0).astype(bf16)
    copies = []
    for half in range(2):
        part = pl.ds(half * (peers // 2), peers // 2)
        rows = dot(hot[half * (slots // 2) : (half + 1) * (slots // 2)], table_ref[...]).astype(bf16)
        rows_ref[part] = rows.reshape(peers // 2, capacity, -1)
        copies.append(pltpu.make_async_copy(rows_ref.at[part], out_ref.at[part], sems.at[half]))
        copies[-1].start()
    for copy in copies:
        copy.wait()


def encode_kernel(pre_ref, placing_ref, rows_ref, second_ref, counts_ref, out_ref, vecs_ref, sems):
    rows = dot(placing_ref[...], rows_ref[...].reshape(placing_ref.shape[1], -1))
    hidden = jnp.maximum(pre_ref[...] + rows, 0.0).astype(bf16)
    emb = dot(hidden, second_ref[...])
    square = jnp.sum(emb * emb, -1, keepdims=True)
    vecs = (emb * lax.rsqrt(square + 1e-06)).astype(bf16)
    n, width = vecs.shape
    bias = jnp.broadcast_to(jnp.log(counts_ref[...].astype(f32)), (extra, n))
    bias = jnp.concatenate([bias] * (width // n), 1).astype(bf16)
    vecs_ref[:n, :] = vecs
    vecs_ref[n:, :] = bias
    peers = out_ref.shape[0]
    copies = [pltpu.make_async_copy(vecs_ref, out_ref.at[i], sems.at[i]) for i in range(peers)]
    for copy in copies:
        copy.start()
    for copy in copies:
        copy.wait()


def bias_row(ref, i, n):
    return ref[i, n : n + extra, :n].astype(f32)[0:1, :] * log2_e


def column(row):
    n = row.shape[1]
    return jnp.sum(jnp.where(iota((n, n), 0) == iota((n, n), 1), row, 0.0), 1, keepdims=True)


def sums(vecs_ref, unit_refs, store):
    peers, width = vecs_ref.shape[0], vecs_ref.shape[2]
    n, rows = vecs_ref.shape[1] - extra, unit_refs[0].shape[1]
    biases = [jnp.broadcast_to(column(bias_row(vecs_ref, i, n)), (n, 128)) for i in range(peers)]
    for t in range(0, 2 * len(unit_refs), 2):
        units = unit_refs[t // 2][...].reshape(2 * rows, width)
        total = jnp.zeros((8, 2 * rows), f32)
        for i in range(0, peers, 2):
            vecs = vecs_ref[i : i + 2, :n, :].reshape(2 * n, width)
            logits = dot(vecs, units, ((1,), (1,)))
            bias = jnp.concatenate([jnp.concatenate(biases[i : i + 2])] * (2 * rows // 128), 1)
            exponent = jnp.exp2(logits * exponent_scale - bias)
            total = total + jnp.sum(exponent.reshape(-1, 8, 2 * rows), 0)
        total = jnp.sum(total, 0, keepdims=True)
        store(t, total[:, :rows])
        store(t + 1, total[:, rows:])


def first_kernel(vecs_ref, ready_ref, *refs):
    out_ref = refs[-1]

    def store(t, value):
        out_ref[t : t + 1, :] = value

    sums(vecs_ref, refs[:-1], store)


def item_sum(place, vecs_ref, units, sums_ref, hot):
    n, width = vecs_ref.shape[1] - extra, vecs_ref.shape[2]
    vecs = vecs_ref[place, :n, :]
    bias = jnp.broadcast_to(column(bias_row(vecs_ref, place, n)), (n, 128))
    grad = jnp.zeros((n, width), f32)
    rows = units[0].shape[1]
    for t in range(2 * len(units)):
        unit = units[t // 2][t % 2]
        exponent = jnp.exp2(
            dot(vecs, unit, ((1,), (1,))) * exponent_scale
            - jnp.concatenate([bias] * (rows // 128), 1)
        )
        residue = exponent * (1.0 / sums_ref[t : t + 1, :])
        if t == 0 and hot is not None:
            residue = residue - hot
        grad += dot(residue.astype(bf16), unit)
    return logit_scale * grad


def second_kernel(place_ref, vecs_ref, first_ref, *refs):
    units, sums_ref, grad_ref = refs[:-2], refs[-2], refs[-1]

    def store(t, value):
        sums_ref[t : t + 1, :] = first_ref[t : t + 1, :] + value

    sums(vecs_ref, units, store)
    grad_ref[...] = item_sum(place_ref[0], vecs_ref, units, sums_ref, None)


def user_kernel(
    place_ref,
    mine_ref,
    other_ref,
    sums_ref,
    users_ref,
    occurrence_ref,
    units_ref,
    loss_ref,
    grad_ref,
    exps,
):
    peers, width = mine_ref.shape[0], mine_ref.shape[2]
    n, rows = mine_ref.shape[1] - extra, users_ref.shape[0]
    place = place_ref[0]
    unit_b = units_ref[0]
    denominator = column(sums_ref[0:1, :])
    inverse = 1.0 / denominator
    occurrence = column(occurrence_ref[...].astype(f32))
    hot = jnp.where(occurrence == iota((rows, n), 1).astype(f32), 1.0, 0.0)
    direction = jnp.zeros((rows, width), f32)
    for half, ref in enumerate((mine_ref, other_ref)):
        for i in range(peers):
            logits = dot(unit_b, ref[i, :n, :], ((1,), (1,))) * exponent_scale
            logits = logits - bias_row(ref, i, n)
            exps[:, i * n : (i + 1) * n] = jnp.exp2(logits) * inverse
        if half == 0:
            own = pl.ds(pl.multiple_of(place * n, n), n)
            exps[:, own] = exps[:, own] - hot
        direction += dot(exps[...].astype(bf16), ref[:, :n, :].reshape(peers * n, width))
    own_logits = dot(unit_b, mine_ref[place, :n, :], ((1,), (1,))) * exponent_scale
    own_logits = own_logits - bias_row(mine_ref, place, n)
    picked = jnp.sum(own_logits * hot, 1, keepdims=True) * (1.0 / log2_e)
    loss = jnp.log(denominator) - picked
    eye = iota((rows, rows), 0) == iota((rows, rows), 1)
    loss_ref[...] = jnp.sum(jnp.where(eye, loss, 0.0), 0, keepdims=True)
    direction = logit_scale * direction
    user_f = users_ref[...].astype(f32)
    scale = lax.rsqrt(jnp.sum(user_f * user_f, -1, keepdims=True) + 1e-06)
    unit = user_f * scale
    grad_ref[...] = scale * (direction - jnp.sum(direction * unit, -1, keepdims=True) * unit)


def item_kernel(place_ref, mine_ref, sums_ref, occurrence_ref, taken_ref, *refs):
    units, out_ref = refs[:-1], refs[-1]
    n, rows = mine_ref.shape[1] - extra, occurrence_ref.shape[1]
    hot = jnp.where(occurrence_ref[...] == iota((n, rows), 0), 1.0, 0.0)
    grad = item_sum(place_ref[0], mine_ref, units, sums_ref, hot)
    out_ref[...] = grad + taken_ref[...]


def shards(item_feats, owner, id_row, counts, occurrence, users, w_first, w_second, id_table):
    n, width = item_feats.shape[0], users.shape[1]
    rows = users.shape[0]
    owners, blocks = lax.axis_size("shard"), lax.axis_size("blk")
    capacity = 2 * n // owners
    slots = owners * capacity
    peers = blocks // 2
    block = lax.axis_index("blk")
    place = block // 2
    swap = [(i, i ^ 1) for i in range(blocks)]

    shape = jax.ShapeDtypeStruct
    long = 10**11
    place_sizes = (
        shape((owners, 128), jnp.int32),
        shape((n, slots), bf16),
        shape((rows, width), bf16),
    )
    ids_sent, placing, payload = call(
        functools.partial(place_kernel, owners, capacity),
        place_sizes,
        8 * n * n * owners,
        4 * owners * 128,
        in_specs=[far_memory] * 3,
        scratch=[
            pltpu.VMEM((1, n), jnp.int32),
            pltpu.VMEM((1, n), jnp.int32),
            pltpu.VMEM((rows, width), bf16),
            pltpu.SemaphoreType.DMA((3,)),
        ],
        room=60,
    )(owner.reshape(1, n), id_row.reshape(1, n), users)
    ids = lax.all_to_all(ids_sent.reshape(owners, 1, 128), "shard", 0, 0, tiled=True)
    table = call(
        table_kernel,
        shape(id_table.shape, bf16),
        long // 20,
        4 * id_table.size,
        in_specs=[far_memory],
        scratch=[pltpu.SemaphoreType.DMA],
    )(id_table)

    def turn(array, step, other_step=None):
        steps = (step, step if other_step is None else other_step)
        pairs = [(i, (i + 2 * steps[i % 2]) % blocks) for i in range(blocks)]
        return lax.ppermute(array, "blk", pairs)

    table_rows = call(
        functools.partial(rows_kernel, capacity),
        shape((owners, capacity, id_table.shape[1]), bf16),
        2 * slots * id_table.size,
        2 * id_table.size,
        scratch=[
            pltpu.VMEM((owners, capacity, id_table.shape[1]), bf16),
            pltpu.SemaphoreType.DMA((2,)),
        ],
        out_specs=far_memory,
    )(ids.reshape(owners, 128), table)
    far = turn(payload, peers // 2)
    table_rows, feats = lax.optimization_barrier((table_rows, item_feats))
    pre = jnp.dot(feats, w_first, preferred_element_type=f32)
    received = lax.all_to_all(table_rows, "shard", 0, 0, tiled=True)
    pair = call(pair_kernel, shape((2, rows, width), bf16), long, 4 * rows * width)(payload, far)
    units = [pair, turn(pair, 1), turn(pair, -1), turn(pair, 2, -2)]
    vecs = call(
        encode_kernel,
        shape((peers, n + extra, width), bf16),
        2 * n * slots * w_first.shape[1],
        2 * received.size,
        scratch=[pltpu.VMEM((n + extra, width), bf16), pltpu.SemaphoreType.DMA((peers,))],
        out_specs=far_memory,
    )(pre, placing, received, w_second, counts.reshape(1, n))

    mine = lax.all_to_all(
        vecs,
        "blk",
        0,
        0,
        axis_index_groups=[list(range(c, blocks, 2)) for c in range(2)],
        tiled=True,
    )
    ready = call(
        ready_kernel, shape((8, 128), f32), long, 1024, in_specs=[pl.BlockSpec(memory_space=pl.ANY)] * 3
    )(*units[1:])
    mine, ready = lax.optimization_barrier((mine, ready))
    other = lax.ppermute(mine, "blk", swap)
    smem = pl.BlockSpec(memory_space=pltpu.SMEM)

    def step(kernel, out_shape, pairs, inputs, scratch=()):
        specs = [smem if i is at else vmem for i in inputs]
        moved = peers * rows * width * 4
        return call(kernel, out_shape, 2 * pairs * width, moved, pairs, specs, scratch, 48)(*inputs)

    at, occurrence = place[None], occurrence.reshape(1, rows)
    pairs = peers * rows * peers * n
    first = step(first_kernel, shape((peers, rows), f32), pairs, (mine, ready, *units))
    total, given = step(
        second_kernel,
        (shape((peers, rows), f32), shape((n, width), f32)),
        pairs,
        (at, other, first, *units),
    )
    taken = lax.ppermute(given, "blk", swap)
    loss, user_grad = step(
        user_kernel,
        (shape((1, rows), f32), shape((rows, width), f32)),
        pairs,
        (at, mine, other, total, users, occurrence, pair),
        [pltpu.VMEM((rows, peers * n), f32)],
    )
    item_grad = step(
        item_kernel,
        shape((n, width), f32),
        peers * rows * n,
        (at, mine, total, occurrence, taken, *units),
    )
    return (loss.reshape(rows), user_grad, item_grad)


def solution(mesh):
    return jax.shard_map(
        shards,
        mesh=mesh,
        in_specs=(
            P(("shard", "blk"), None),
            P(("shard", "blk"), None),
            P(("shard", "blk")),
            P(("shard", "blk")),
            P(("shard", "blk")),
            P(("shard", "blk"), None),
            P(),
            P(),
            P("shard", None),
        ),
        out_specs=(P(("shard", "blk")), P(("shard", "blk"), None), P(("shard", "blk"), None)),
        check_vma=False,
    )
```

```python
import functools

import jax
import jax.numpy as jnp
from jax import lax
from jax.experimental import pallas as pl
from jax.experimental.pallas import tpu as pltpu
from jax.sharding import PartitionSpec as P

logit_scale = 48.0
log2_e = 1.4426950408889634
exponent_scale = logit_scale * log2_e
vmem = pl.BlockSpec(memory_space=pltpu.VMEM)
far_memory = pl.BlockSpec(memory_space=pltpu.HBM)
anywhere = pl.BlockSpec(memory_space=pl.ANY)
f32, bf16 = jnp.float32, jnp.bfloat16
extra = 8


def call(kernel, out_shape, flops, moved, exps=0, in_specs=None, scratch=(), room=16, out_specs=None):
    if out_specs is None:
        out_specs = [vmem] * len(out_shape) if isinstance(out_shape, tuple) else vmem
    options = {} if in_specs is None else {"in_specs": in_specs}
    return pl.pallas_call(
        kernel,
        out_shape=out_shape,
        out_specs=out_specs,
        scratch_shapes=scratch,
        compiler_params=pltpu.CompilerParams(vmem_limit_bytes=room * 2**20),
        cost_estimate=pl.CostEstimate(flops=flops, bytes_accessed=moved, transcendentals=exps),
        **options,
    )


def dot(a, b, contract=((1,), (0,))):
    return lax.dot_general(a, b, (contract, ((), ())), preferred_element_type=f32)


def iota(shape, dim):
    return lax.broadcasted_iota(jnp.int32, shape, dim)


def place_kernel(
    owners,
    capacity,
    owner_in,
    id_in,
    users_in,
    ids_ref,
    placing_ref,
    payload_ref,
    owner_ref,
    id_ref,
    users_ref,
    sems,
):
    pairs = (owner_in, owner_ref), (id_in, id_ref), (users_in, users_ref)
    copies = [pltpu.make_async_copy(*pair, sems.at[i]) for i, pair in enumerate(pairs)]
    for copy in copies:
        copy.start()
    for copy in copies:
        copy.wait()
    n = owner_ref.shape[1]
    eye = iota((n, n), 0) == iota((n, n), 1)
    owner = jnp.sum(jnp.where(eye, owner_ref[...], 0).astype(f32), 1, keepdims=True)
    ids = jnp.sum(jnp.where(eye, id_ref[...], 0).astype(f32), 1, keepdims=True)
    hot = jnp.where(owner == iota((n, owners), 1).astype(f32), 1.0, 0.0)
    earlier = jnp.where(iota((n, n), 0) > iota((n, n), 1), 1.0, 0.0).astype(bf16)
    before = dot(earlier, hot.astype(bf16))
    rank = jnp.sum(before * hot, 1, keepdims=True)
    high = jnp.floor(ids * (1.0 / 32.0))
    low = ids - 32.0 * high
    lane = iota((n, 128), 1).astype(f32)
    parts = jnp.where(lane == rank, high, 0.0) + jnp.where(lane == rank + capacity, low, 0.0)
    ids_ref[...] = dot(hot.astype(bf16), parts.astype(bf16), ((0,), (0,))).astype(jnp.int32)
    position = owner * capacity + rank
    placing_ref[...] = jnp.where(
        position == iota((n, owners * capacity), 1).astype(f32), 1.0, 0.0
    ).astype(bf16)
    user_f = users_ref[...].astype(f32)
    inverse = lax.rsqrt(jnp.sum(user_f * user_f, -1, keepdims=True) + 1e-06)
    payload_ref[...] = (user_f * inverse).astype(bf16)


def early_kernel(payload_ref, out_ref):
    out_ref[...] = jnp.zeros_like(out_ref)


def table_kernel(table_in, after_ref, table_ref, sem):
    copy = pltpu.make_async_copy(table_in, table_ref, sem)
    copy.start()
    copy.wait()


def pair_kernel(near_ref, far_ref, out_ref):
    out_ref[0] = near_ref[...]
    out_ref[1] = far_ref[...]


def ready_kernel(one_ref, two_ref, three_ref, out_ref):
    out_ref[...] = jnp.zeros_like(out_ref)


def rows_kernel(capacity, ids_ref, table_ref, out_ref, rows_ref, sems):
    peers = ids_ref.shape[0]
    slots = peers * capacity
    peer_of = iota((slots, peers), 0) // capacity
    spread = jnp.where(peer_of == iota((slots, peers), 1), 1.0, 0.0).astype(bf16)
    parts = dot(spread, ids_ref[...].astype(bf16))
    lane, slot = iota((slots, 128), 1), iota((slots, 128), 0) % capacity
    weight = jnp.where(lane == slot, 32.0, 0.0) + jnp.where(lane == slot + capacity, 1.0, 0.0)
    ids = jnp.sum(parts * weight, 1, keepdims=True)
    hot = jnp.where(ids == iota((slots, table_ref.shape[0]), 1).astype(f32), 1.0, 0.0).astype(bf16)
    copies = []
    for half in range(2):
        part = pl.ds(half * (peers // 2), peers // 2)
        rows = dot(hot[half * (slots // 2) : (half + 1) * (slots // 2)], table_ref[...]).astype(bf16)
        rows_ref[part] = rows.reshape(peers // 2, capacity, -1)
        copies.append(pltpu.make_async_copy(rows_ref.at[part], out_ref.at[part], sems.at[half]))
        copies[-1].start()
    for copy in copies:
        copy.wait()


def encode_kernel(pre_ref, placing_ref, rows_ref, second_ref, counts_ref, out_ref, vecs_ref, sems):
    rows = dot(placing_ref[...], rows_ref[...].reshape(placing_ref.shape[1], -1))
    hidden = jnp.maximum(pre_ref[...] + rows, 0.0).astype(bf16)
    emb = dot(hidden, second_ref[...])
    square = jnp.sum(emb * emb, -1, keepdims=True)
    vecs = (emb * lax.rsqrt(square + 1e-06)).astype(bf16)
    n, width = vecs.shape
    bias = jnp.broadcast_to(jnp.log(counts_ref[...].astype(f32)), (extra, n))
    bias = jnp.concatenate([bias] * (width // n), 1).astype(bf16)
    vecs_ref[:n, :] = vecs
    vecs_ref[n:, :] = bias
    peers = out_ref.shape[0]
    copies = [pltpu.make_async_copy(vecs_ref, out_ref.at[i], sems.at[i]) for i in range(peers)]
    for copy in copies:
        copy.start()
    for copy in copies:
        copy.wait()


def bias_row(ref, i, n):
    return ref[i, n : n + extra, :n].astype(f32)[0:1, :] * log2_e


def column(row):
    n = row.shape[1]
    return jnp.sum(jnp.where(iota((n, n), 0) == iota((n, n), 1), row, 0.0), 1, keepdims=True)


def sums(vecs_ref, unit_refs, store):
    peers, width = vecs_ref.shape[0], vecs_ref.shape[2]
    n, rows = vecs_ref.shape[1] - extra, unit_refs[0].shape[1]
    biases = [jnp.broadcast_to(column(bias_row(vecs_ref, i, n)), (n, 128)) for i in range(peers)]
    for t in range(0, 2 * len(unit_refs), 2):
        units = unit_refs[t // 2][...].reshape(2 * rows, width)
        total = jnp.zeros((8, 2 * rows), f32)
        for i in range(0, peers, 2):
            vecs = vecs_ref[i : i + 2, :n, :].reshape(2 * n, width)
            logits = dot(vecs, units, ((1,), (1,)))
            bias = jnp.concatenate([jnp.concatenate(biases[i : i + 2])] * (2 * rows // 128), 1)
            exponent = jnp.exp2(logits * exponent_scale - bias)
            total = total + jnp.sum(exponent.reshape(-1, 8, 2 * rows), 0)
        total = jnp.sum(total, 0, keepdims=True)
        store(t, total[:, :rows])
        store(t + 1, total[:, rows:])


def first_kernel(vecs_ref, ready_ref, *refs):
    out_ref = refs[-1]

    def store(t, value):
        out_ref[t : t + 1, :] = value

    sums(vecs_ref, refs[:-1], store)


def item_sum(place, vecs_ref, units, sums_ref, hot):
    n, width = vecs_ref.shape[1] - extra, vecs_ref.shape[2]
    vecs = vecs_ref[place, :n, :]
    bias = jnp.broadcast_to(column(bias_row(vecs_ref, place, n)), (n, 128))
    grad = jnp.zeros((n, width), f32)
    rows = units[0].shape[1]
    for t in range(2 * len(units)):
        unit = units[t // 2][t % 2]
        exponent = jnp.exp2(
            dot(vecs, unit, ((1,), (1,))) * exponent_scale
            - jnp.concatenate([bias] * (rows // 128), 1)
        )
        residue = exponent * (1.0 / sums_ref[t : t + 1, :])
        if t == 0 and hot is not None:
            residue = residue - hot
        grad += dot(residue.astype(bf16), unit)
    return logit_scale * grad


def second_kernel(place_ref, vecs_ref, first_ref, *refs):
    units, sums_ref, grad_ref = refs[:-2], refs[-2], refs[-1]

    def store(t, value):
        sums_ref[t : t + 1, :] = first_ref[t : t + 1, :] + value

    sums(vecs_ref, units, store)
    grad_ref[...] = item_sum(place_ref[0], vecs_ref, units, sums_ref, None)


def user_kernel(
    place_ref,
    mine_ref,
    other_ref,
    sums_ref,
    users_ref,
    occurrence_ref,
    units_ref,
    loss_ref,
    grad_ref,
    exps,
):
    peers, width = mine_ref.shape[0], mine_ref.shape[2]
    n, rows = mine_ref.shape[1] - extra, users_ref.shape[0]
    place = place_ref[0]
    unit_b = units_ref[0]
    denominator = column(sums_ref[0:1, :])
    inverse = 1.0 / denominator
    occurrence = column(occurrence_ref[...].astype(f32))
    hot = jnp.where(occurrence == iota((rows, n), 1).astype(f32), 1.0, 0.0)
    direction = jnp.zeros((rows, width), f32)
    for half, ref in enumerate((mine_ref, other_ref)):
        for i in range(peers):
            logits = dot(unit_b, ref[i, :n, :], ((1,), (1,))) * exponent_scale
            logits = logits - bias_row(ref, i, n)
            exps[:, i * n : (i + 1) * n] = jnp.exp2(logits) * inverse
        if half == 0:
            own = pl.ds(pl.multiple_of(place * n, n), n)
            exps[:, own] = exps[:, own] - hot
        direction += dot(exps[...].astype(bf16), ref[:, :n, :].reshape(peers * n, width))
    own_logits = dot(unit_b, mine_ref[place, :n, :], ((1,), (1,))) * exponent_scale
    own_logits = own_logits - bias_row(mine_ref, place, n)
    picked = jnp.sum(own_logits * hot, 1, keepdims=True) * (1.0 / log2_e)
    loss = jnp.log(denominator) - picked
    eye = iota((rows, rows), 0) == iota((rows, rows), 1)
    loss_ref[...] = jnp.sum(jnp.where(eye, loss, 0.0), 0, keepdims=True)
    direction = logit_scale * direction
    user_f = users_ref[...].astype(f32)
    scale = lax.rsqrt(jnp.sum(user_f * user_f, -1, keepdims=True) + 1e-06)
    unit = user_f * scale
    grad_ref[...] = scale * (direction - jnp.sum(direction * unit, -1, keepdims=True) * unit)


def item_kernel(place_ref, mine_ref, sums_ref, occurrence_ref, taken_ref, *refs):
    units, out_ref = refs[:-1], refs[-1]
    n, rows = mine_ref.shape[1] - extra, occurrence_ref.shape[1]
    hot = jnp.where(occurrence_ref[...] == iota((n, rows), 0), 1.0, 0.0)
    grad = item_sum(place_ref[0], mine_ref, units, sums_ref, hot)
    out_ref[...] = grad + taken_ref[...]


def shards(item_feats, owner, id_row, counts, occurrence, users, w_first, w_second, id_table):
    n, width = item_feats.shape[0], users.shape[1]
    rows = users.shape[0]
    owners, blocks = lax.axis_size("shard"), lax.axis_size("blk")
    capacity = 2 * n // owners
    slots = owners * capacity
    peers = blocks // 2
    block = lax.axis_index("blk")
    place = block // 2
    swap = [(i, i ^ 1) for i in range(blocks)]

    shape = jax.ShapeDtypeStruct
    long = 10**11
    place_sizes = (
        shape((owners, 128), jnp.int32),
        shape((n, slots), bf16),
        shape((rows, width), bf16),
    )
    ids_sent, placing, payload = call(
        functools.partial(place_kernel, owners, capacity),
        place_sizes,
        8 * n * n * owners,
        4 * owners * 128,
        in_specs=[far_memory] * 3,
        scratch=[
            pltpu.VMEM((1, n), jnp.int32),
            pltpu.VMEM((1, n), jnp.int32),
            pltpu.VMEM((rows, width), bf16),
            pltpu.SemaphoreType.DMA((3,)),
        ],
        room=60,
    )(owner.reshape(1, n), id_row.reshape(1, n), users)
    ids = lax.all_to_all(ids_sent.reshape(owners, 1, 128), "shard", 0, 0, tiled=True)
    early = call(early_kernel, shape((8, 128), f32), long // 20, 1024, in_specs=[anywhere])(payload)
    table = call(
        table_kernel,
        shape(id_table.shape, bf16),
        long // 20,
        4 * id_table.size,
        in_specs=[far_memory, anywhere],
        scratch=[pltpu.SemaphoreType.DMA],
    )(id_table, early)

    def turn(array, step, other_step=None):
        steps = (step, step if other_step is None else other_step)
        pairs = [(i, (i + 2 * steps[i % 2]) % blocks) for i in range(blocks)]
        return lax.ppermute(array, "blk", pairs)

    table_rows = call(
        functools.partial(rows_kernel, capacity),
        shape((owners, capacity, id_table.shape[1]), bf16),
        2 * slots * id_table.size,
        2 * id_table.size,
        scratch=[
            pltpu.VMEM((owners, capacity, id_table.shape[1]), bf16),
            pltpu.SemaphoreType.DMA((2,)),
        ],
        out_specs=far_memory,
    )(ids.reshape(owners, 128), table)
    far = turn(payload, peers // 2)
    table_rows, feats = lax.optimization_barrier((table_rows, item_feats))
    pre = jnp.dot(feats, w_first, preferred_element_type=f32)
    received = lax.all_to_all(table_rows, "shard", 0, 0, tiled=True)
    pair = call(pair_kernel, shape((2, rows, width), bf16), long, 4 * rows * width)(payload, far)
    units = [pair, turn(pair, 1), turn(pair, -1), turn(pair, 2, -2)]
    vecs = call(
        encode_kernel,
        shape((peers, n + extra, width), bf16),
        2 * n * slots * w_first.shape[1],
        2 * received.size,
        scratch=[pltpu.VMEM((n + extra, width), bf16), pltpu.SemaphoreType.DMA((peers,))],
        out_specs=far_memory,
    )(pre, placing, received, w_second, counts.reshape(1, n))

    mine = lax.all_to_all(
        vecs,
        "blk",
        0,
        0,
        axis_index_groups=[list(range(c, blocks, 2)) for c in range(2)],
        tiled=True,
    )
    ready = call(
        ready_kernel, shape((8, 128), f32), long, 1024, in_specs=[anywhere] * 3
    )(*units[1:])
    mine, ready = lax.optimization_barrier((mine, ready))
    other = lax.ppermute(mine, "blk", swap)
    smem = pl.BlockSpec(memory_space=pltpu.SMEM)

    def step(kernel, out_shape, pairs, inputs, scratch=()):
        specs = [smem if i is at else vmem for i in inputs]
        moved = peers * rows * width * 4
        return call(kernel, out_shape, 2 * pairs * width, moved, pairs, specs, scratch, 48)(*inputs)

    at, occurrence = place[None], occurrence.reshape(1, rows)
    pairs = peers * rows * peers * n
    first = step(first_kernel, shape((peers, rows), f32), pairs, (mine, ready, *units))
    total, given = step(
        second_kernel,
        (shape((peers, rows), f32), shape((n, width), f32)),
        pairs,
        (at, other, first, *units),
    )
    taken = lax.ppermute(given, "blk", swap)
    loss, user_grad = step(
        user_kernel,
        (shape((1, rows), f32), shape((rows, width), f32)),
        pairs,
        (at, mine, other, total, users, occurrence, pair),
        [pltpu.VMEM((rows, peers * n), f32)],
    )
    item_grad = step(
        item_kernel,
        shape((n, width), f32),
        peers * rows * n,
        (at, mine, total, occurrence, taken, *units),
    )
    return (loss.reshape(rows), user_grad, item_grad)


def solution(mesh):
    return jax.shard_map(
        shards,
        mesh=mesh,
        in_specs=(
            P(("shard", "blk"), None),
            P(("shard", "blk"), None),
            P(("shard", "blk")),
            P(("shard", "blk")),
            P(("shard", "blk")),
            P(("shard", "blk"), None),
            P(),
            P(),
            P("shard", None),
        ),
        out_specs=(P(("shard", "blk")), P(("shard", "blk"), None), P(("shard", "blk"), None)),
        check_vma=False,
    )
```

```python
import functools

import jax
import jax.numpy as jnp
from jax import lax
from jax.experimental import pallas as pl
from jax.experimental.pallas import tpu as pltpu
from jax.sharding import PartitionSpec as P

logit_scale = 48.0
log2_e = 1.4426950408889634
exponent_scale = logit_scale * log2_e
vmem = pl.BlockSpec(memory_space=pltpu.VMEM)
far_memory = pl.BlockSpec(memory_space=pltpu.HBM)
anywhere = pl.BlockSpec(memory_space=pl.ANY)
f32, bf16 = jnp.float32, jnp.bfloat16
extra = 16


def call(kernel, out_shape, flops, moved, exps=0, in_specs=None, scratch=(), room=16, out_specs=None):
    if out_specs is None:
        out_specs = [vmem] * len(out_shape) if isinstance(out_shape, tuple) else vmem
    options = {} if in_specs is None else {"in_specs": in_specs}
    return pl.pallas_call(
        kernel,
        out_shape=out_shape,
        out_specs=out_specs,
        scratch_shapes=scratch,
        compiler_params=pltpu.CompilerParams(vmem_limit_bytes=room * 2**20),
        cost_estimate=pl.CostEstimate(flops=flops, bytes_accessed=moved, transcendentals=exps),
        **options,
    )


def dot(a, b, contract=((1,), (0,))):
    return lax.dot_general(a, b, (contract, ((), ())), preferred_element_type=f32)


def iota(shape, dim):
    return lax.broadcasted_iota(jnp.int32, shape, dim)


def place_kernel(
    owners,
    capacity,
    owner_in,
    id_in,
    users_in,
    ids_ref,
    placing_ref,
    payload_ref,
    owner_ref,
    id_ref,
    users_ref,
    sems,
):
    pairs = (owner_in, owner_ref), (id_in, id_ref), (users_in, users_ref)
    copies = [pltpu.make_async_copy(*pair, sems.at[i]) for i, pair in enumerate(pairs)]
    for copy in copies:
        copy.start()
    for copy in copies:
        copy.wait()
    n = owner_ref.shape[1]
    eye = iota((n, n), 0) == iota((n, n), 1)
    owner = jnp.sum(jnp.where(eye, owner_ref[...], 0).astype(f32), 1, keepdims=True)
    ids = jnp.sum(jnp.where(eye, id_ref[...], 0).astype(f32), 1, keepdims=True)
    hot = jnp.where(owner == iota((n, owners), 1).astype(f32), 1.0, 0.0)
    earlier = jnp.where(iota((n, n), 0) > iota((n, n), 1), 1.0, 0.0).astype(bf16)
    before = dot(earlier, hot.astype(bf16))
    rank = jnp.sum(before * hot, 1, keepdims=True)
    high = jnp.floor(ids * (1.0 / 32.0))
    low = ids - 32.0 * high
    lane = iota((n, 128), 1).astype(f32)
    parts = jnp.where(lane == rank, high, 0.0) + jnp.where(lane == rank + capacity, low, 0.0)
    ids_ref[...] = dot(hot.astype(bf16), parts.astype(bf16), ((0,), (0,))).astype(jnp.int32)
    position = owner * capacity + rank
    placing_ref[...] = jnp.where(
        position == iota((n, owners * capacity), 1).astype(f32), 1.0, 0.0
    ).astype(bf16)
    user_f = users_ref[...].astype(f32)
    inverse = lax.rsqrt(jnp.sum(user_f * user_f, -1, keepdims=True) + 1e-06)
    payload_ref[...] = (user_f * inverse).astype(bf16)


def early_kernel(payload_ref, out_ref):
    out_ref[...] = jnp.zeros_like(out_ref)


def table_kernel(table_in, after_ref, table_ref, sem):
    copy = pltpu.make_async_copy(table_in, table_ref, sem)
    copy.start()
    copy.wait()


def pair_kernel(near_ref, far_ref, out_ref):
    out_ref[0] = near_ref[...]
    out_ref[1] = far_ref[...]


def ready_kernel(one_ref, two_ref, three_ref, out_ref):
    out_ref[...] = jnp.zeros_like(out_ref)


def rows_kernel(capacity, ids_ref, table_ref, out_ref, rows_ref, sems):
    peers = ids_ref.shape[0]
    slots = peers * capacity
    peer_of = iota((slots, peers), 0) // capacity
    spread = jnp.where(peer_of == iota((slots, peers), 1), 1.0, 0.0).astype(bf16)
    parts = dot(spread, ids_ref[...].astype(bf16))
    lane, slot = iota((slots, 128), 1), iota((slots, 128), 0) % capacity
    weight = jnp.where(lane == slot, 32.0, 0.0) + jnp.where(lane == slot + capacity, 1.0, 0.0)
    ids = jnp.sum(parts * weight, 1, keepdims=True)
    hot = jnp.where(ids == iota((slots, table_ref.shape[0]), 1).astype(f32), 1.0, 0.0).astype(bf16)
    copies = []
    for half in range(2):
        part = pl.ds(half * (peers // 2), peers // 2)
        rows = dot(hot[half * (slots // 2) : (half + 1) * (slots // 2)], table_ref[...]).astype(bf16)
        rows_ref[part] = rows.reshape(peers // 2, capacity, -1)
        copies.append(pltpu.make_async_copy(rows_ref.at[part], out_ref.at[part], sems.at[half]))
        copies[-1].start()
    for copy in copies:
        copy.wait()


def encode_kernel(pre_ref, placing_ref, rows_ref, second_ref, counts_ref, out_ref, vecs_ref, sems):
    rows = dot(placing_ref[...], rows_ref[...].reshape(placing_ref.shape[1], -1))
    hidden = jnp.maximum(pre_ref[...] + rows, 0.0).astype(bf16)
    emb = dot(hidden, second_ref[...])
    square = jnp.sum(emb * emb, -1, keepdims=True)
    vecs = (emb * lax.rsqrt(square + 1e-06)).astype(bf16)
    n, width = vecs.shape
    bias = jnp.broadcast_to(jnp.log(counts_ref[...].astype(f32)), (extra, n))
    bias = jnp.concatenate([bias] * (width // n), 1).astype(bf16)
    vecs_ref[:n, :] = vecs
    vecs_ref[n:, :] = bias
    peers = out_ref.shape[0]
    copies = [pltpu.make_async_copy(vecs_ref, out_ref.at[i], sems.at[i]) for i in range(peers)]
    for copy in copies:
        copy.start()
    for copy in copies:
        copy.wait()


def bias_row(ref, i, n):
    return ref[i, n : n + extra, :n].astype(f32)[0:1, :] * log2_e


def column(row):
    n = row.shape[1]
    return jnp.sum(jnp.where(iota((n, n), 0) == iota((n, n), 1), row, 0.0), 1, keepdims=True)


def sums(vecs_ref, unit_refs, store):
    peers, width = vecs_ref.shape[0], vecs_ref.shape[2]
    n, rows = vecs_ref.shape[1] - extra, unit_refs[0].shape[1]
    biases = [jnp.broadcast_to(column(bias_row(vecs_ref, i, n)), (n, 128)) for i in range(peers)]
    for t in range(0, 2 * len(unit_refs), 2):
        units = unit_refs[t // 2][...].reshape(2 * rows, width)
        total = jnp.zeros((8, 2 * rows), f32)
        for i in range(0, peers, 2):
            vecs = vecs_ref[i : i + 2, :n, :].reshape(2 * n, width)
            logits = dot(vecs, units, ((1,), (1,)))
            bias = jnp.concatenate([jnp.concatenate(biases[i : i + 2])] * (2 * rows // 128), 1)
            exponent = jnp.exp2(logits * exponent_scale - bias)
            total = total + jnp.sum(exponent.reshape(-1, 8, 2 * rows), 0)
        total = jnp.sum(total, 0, keepdims=True)
        store(t, total[:, :rows])
        store(t + 1, total[:, rows:])


def first_kernel(vecs_ref, ready_ref, *refs):
    out_ref = refs[-1]

    def store(t, value):
        out_ref[t : t + 1, :] = value

    sums(vecs_ref, refs[:-1], store)


def item_sum(place, vecs_ref, units, sums_ref, hot):
    n, width = vecs_ref.shape[1] - extra, vecs_ref.shape[2]
    vecs = vecs_ref[place, :n, :]
    bias = jnp.broadcast_to(column(bias_row(vecs_ref, place, n)), (n, 128))
    grad = jnp.zeros((n, width), f32)
    rows = units[0].shape[1]
    for t in range(2 * len(units)):
        unit = units[t // 2][t % 2]
        exponent = jnp.exp2(
            dot(vecs, unit, ((1,), (1,))) * exponent_scale
            - jnp.concatenate([bias] * (rows // 128), 1)
        )
        residue = exponent * (1.0 / sums_ref[t : t + 1, :])
        if t == 0 and hot is not None:
            residue = residue - hot
        grad += dot(residue.astype(bf16), unit)
    return logit_scale * grad


def second_kernel(place_ref, vecs_ref, first_ref, *refs):
    units, sums_ref, grad_ref = refs[:-2], refs[-2], refs[-1]

    def store(t, value):
        sums_ref[t : t + 1, :] = first_ref[t : t + 1, :] + value

    sums(vecs_ref, units, store)
    grad_ref[...] = item_sum(place_ref[0], vecs_ref, units, sums_ref, None)


def user_kernel(
    place_ref,
    mine_ref,
    other_ref,
    sums_ref,
    users_ref,
    occurrence_ref,
    units_ref,
    loss_ref,
    grad_ref,
    exps,
):
    peers, width = mine_ref.shape[0], mine_ref.shape[2]
    n, rows = mine_ref.shape[1] - extra, users_ref.shape[0]
    place = place_ref[0]
    unit_b = units_ref[0]
    denominator = column(sums_ref[0:1, :])
    inverse = 1.0 / denominator
    occurrence = column(occurrence_ref[...].astype(f32))
    hot = jnp.where(occurrence == iota((rows, n), 1).astype(f32), 1.0, 0.0)
    direction = jnp.zeros((rows, width), f32)
    for half, ref in enumerate((mine_ref, other_ref)):
        for i in range(peers):
            logits = dot(unit_b, ref[i, :n, :], ((1,), (1,))) * exponent_scale
            logits = logits - bias_row(ref, i, n)
            exps[:, i * n : (i + 1) * n] = jnp.exp2(logits) * inverse
        if half == 0:
            own = pl.ds(pl.multiple_of(place * n, n), n)
            exps[:, own] = exps[:, own] - hot
        direction += dot(exps[...].astype(bf16), ref[:, :n, :].reshape(peers * n, width))
    own_logits = dot(unit_b, mine_ref[place, :n, :], ((1,), (1,))) * exponent_scale
    own_logits = own_logits - bias_row(mine_ref, place, n)
    picked = jnp.sum(own_logits * hot, 1, keepdims=True) * (1.0 / log2_e)
    loss = jnp.log(denominator) - picked
    eye = iota((rows, rows), 0) == iota((rows, rows), 1)
    loss_ref[...] = jnp.sum(jnp.where(eye, loss, 0.0), 0, keepdims=True)
    direction = logit_scale * direction
    user_f = users_ref[...].astype(f32)
    scale = lax.rsqrt(jnp.sum(user_f * user_f, -1, keepdims=True) + 1e-06)
    unit = user_f * scale
    grad_ref[...] = scale * (direction - jnp.sum(direction * unit, -1, keepdims=True) * unit)


def item_kernel(place_ref, mine_ref, sums_ref, occurrence_ref, taken_ref, *refs):
    units, out_ref = refs[:-1], refs[-1]
    n, rows = mine_ref.shape[1] - extra, occurrence_ref.shape[1]
    hot = jnp.where(occurrence_ref[...] == iota((n, rows), 0), 1.0, 0.0)
    grad = item_sum(place_ref[0], mine_ref, units, sums_ref, hot)
    out_ref[...] = grad + taken_ref[...]


def shards(item_feats, owner, id_row, counts, occurrence, users, w_first, w_second, id_table):
    n, width = item_feats.shape[0], users.shape[1]
    rows = users.shape[0]
    owners, blocks = lax.axis_size("shard"), lax.axis_size("blk")
    capacity = 2 * n // owners
    slots = owners * capacity
    peers = blocks // 2
    block = lax.axis_index("blk")
    place = block // 2
    swap = [(i, i ^ 1) for i in range(blocks)]

    shape = jax.ShapeDtypeStruct
    long = 10**11
    place_sizes = (
        shape((owners, 128), jnp.int32),
        shape((n, slots), bf16),
        shape((rows, width), bf16),
    )
    ids_sent, placing, payload = call(
        functools.partial(place_kernel, owners, capacity),
        place_sizes,
        8 * n * n * owners,
        4 * owners * 128,
        in_specs=[far_memory] * 3,
        scratch=[
            pltpu.VMEM((1, n), jnp.int32),
            pltpu.VMEM((1, n), jnp.int32),
            pltpu.VMEM((rows, width), bf16),
            pltpu.SemaphoreType.DMA((3,)),
        ],
        room=60,
    )(owner.reshape(1, n), id_row.reshape(1, n), users)
    ids = lax.all_to_all(ids_sent.reshape(owners, 1, 128), "shard", 0, 0, tiled=True)
    early = call(early_kernel, shape((8, 128), f32), long // 20, 1024, in_specs=[anywhere])(payload)
    table = call(
        table_kernel,
        shape(id_table.shape, bf16),
        long // 20,
        4 * id_table.size,
        in_specs=[far_memory, anywhere],
        scratch=[pltpu.SemaphoreType.DMA],
    )(id_table, early)

    def turn(array, step, other_step=None):
        steps = (step, step if other_step is None else other_step)
        pairs = [(i, (i + 2 * steps[i % 2]) % blocks) for i in range(blocks)]
        return lax.ppermute(array, "blk", pairs)

    table_rows = call(
        functools.partial(rows_kernel, capacity),
        shape((owners, capacity, id_table.shape[1]), bf16),
        2 * slots * id_table.size,
        2 * id_table.size,
        scratch=[
            pltpu.VMEM((owners, capacity, id_table.shape[1]), bf16),
            pltpu.SemaphoreType.DMA((2,)),
        ],
        out_specs=far_memory,
    )(ids.reshape(owners, 128), table)
    far = turn(payload, peers // 2)
    table_rows, feats = lax.optimization_barrier((table_rows, item_feats))
    pre = jnp.dot(feats, w_first, preferred_element_type=f32)
    received = lax.all_to_all(table_rows, "shard", 0, 0, tiled=True)
    pair = call(pair_kernel, shape((2, rows, width), bf16), long, 4 * rows * width)(payload, far)
    units = [pair, turn(pair, 1), turn(pair, -1), turn(pair, 2, -2)]
    vecs = call(
        encode_kernel,
        shape((peers, n + extra, width), bf16),
        2 * n * slots * w_first.shape[1],
        2 * received.size,
        scratch=[pltpu.VMEM((n + extra, width), bf16), pltpu.SemaphoreType.DMA((peers,))],
        out_specs=far_memory,
    )(pre, placing, received, w_second, counts.reshape(1, n))

    mine = lax.all_to_all(
        vecs,
        "blk",
        0,
        0,
        axis_index_groups=[list(range(c, blocks, 2)) for c in range(2)],
        tiled=True,
    )
    ready = call(
        ready_kernel, shape((8, 128), f32), long, 1024, in_specs=[anywhere] * 3
    )(*units[1:])
    mine, ready = lax.optimization_barrier((mine, ready))
    other = lax.ppermute(mine, "blk", swap)
    smem = pl.BlockSpec(memory_space=pltpu.SMEM)

    def step(kernel, out_shape, pairs, inputs, scratch=()):
        specs = [smem if i is at else vmem for i in inputs]
        moved = peers * rows * width * 4
        return call(kernel, out_shape, 2 * pairs * width, moved, pairs, specs, scratch, 48)(*inputs)

    at, occurrence = place[None], occurrence.reshape(1, rows)
    pairs = peers * rows * peers * n
    first = step(first_kernel, shape((peers, rows), f32), pairs, (mine, ready, *units))
    total, given = step(
        second_kernel,
        (shape((peers, rows), f32), shape((n, width), f32)),
        pairs,
        (at, other, first, *units),
    )
    taken = lax.ppermute(given, "blk", swap)
    loss, user_grad = step(
        user_kernel,
        (shape((1, rows), f32), shape((rows, width), f32)),
        pairs,
        (at, mine, other, total, users, occurrence, pair),
        [pltpu.VMEM((rows, peers * n), f32)],
    )
    item_grad = step(
        item_kernel,
        shape((n, width), f32),
        peers * rows * n,
        (at, mine, total, occurrence, taken, *units),
    )
    return (loss.reshape(rows), user_grad, item_grad)


def solution(mesh):
    return jax.shard_map(
        shards,
        mesh=mesh,
        in_specs=(
            P(("shard", "blk"), None),
            P(("shard", "blk"), None),
            P(("shard", "blk")),
            P(("shard", "blk")),
            P(("shard", "blk")),
            P(("shard", "blk"), None),
            P(),
            P(),
            P("shard", None),
        ),
        out_specs=(P(("shard", "blk")), P(("shard", "blk"), None), P(("shard", "blk"), None)),
        check_vma=False,
    )
```
